32 devices in a mesh: beam: 4 (over z), lat: 8 (over y, x, core).
Axes of the slice: x: 2, y: 2, z: 4, core: 2. Of those that a mesh axis runs over, the one named last changes fastest.
Arguments:
- contrast: float32 [2, 4, 1024, 256], P(None, 'beam', 'lat'), may hold values from -0.15 to 0.15
- probe: float32 [2, 128, 128], replicated, may hold values from -6 to 6
- offset_x: int32 [64], P('lat'), may hold values from 0 to 127
- offset_y: int32 [64], P('lat'), may hold values from 0 to 128
- probe_count: int32 [8], P('lat'), may hold values from 1 to 8, 48 in all
- measured: float32 [64, 128, 128], P('lat'), may hold values from 0 to 4
Outputs:
- object_gradient: float32 [2, 4, 1024, 256], P(None, 'beam', 'lat')
The draws below stay inside these ranges and needn't reach their ends.
Inputs may be any that keep to these rules, and one draw needn't show every extreme that they name: `probe_count`: slots below this count hold probes; the others hold none and add nothing; some lat index has all 8. `offset_x`: a probe's block may reach into the next lat index's columns.
All inputs are finite; a program needn't handle non-finite values. No bound on the sum of `probe_count` on one device may be relied on, other than what follows from the above.
Results may differ from the reference program's by a relative error of at most 0.038.
Values may be sent and summed in bfloat16 or wider, within the bound.
No kernel may reach another device: no remote copies, remote signals or barrier semaphores. Data moves between devices by JAX's collectives and lax.ppermute only.
A program may use at most 64 MiB of HBM per device.

```python
import math
import jax
import jax.numpy as jnp
import numpy as np
from jax import lax

PATCH = 128
SLICES = 1
TILE = 128
HEIGHT = 256
SLOTS = 8
NZ = 4
NX = 1024
PROBES = 64
N_BEAM = 4
N_LAT = 8


def with_ends(drawn, key, smallest, largest):
    extent = drawn.shape
    spot = [jax.random.randint(jax.random.fold_in(key, axis), (), 0, extent[axis]) for axis in range(len(extent))]
    drawn = drawn.at[tuple(spot)].set(smallest)
    longest = extent.index(max(extent))
    spot[longest] = (spot[longest] + 1) % extent[longest]
    return drawn.at[tuple(spot)].set(largest)


def block_levels(stream_key, extent, cuts, least, high):
    def one(dim, blocks):
        steps = jax.random.uniform(jax.random.fold_in(jax.random.fold_in(stream_key, 6), dim), (blocks,), jnp.float32, least / len(cuts), high / len(cuts))
        return jnp.repeat(jnp.exp(steps), extent[dim] // blocks).reshape((-1,) + (1,) * (len(extent) - dim - 1))

    gain = one(*cuts[0])
    for cut in cuts[1:]:
        gain = gain * one(*cut)
    return gain


def split_up(number_of, total, limit, lean):
    loads = [(1 << 20) // math.isqrt(standing ** lean) + 1 for standing in range(2, number_of + 1)]
    spare, counts = total - limit - (number_of - 1), [1] * (number_of - 1)
    while spare > 0:
        candidates = [i for i in range(number_of - 1) if counts[i] < limit]
        pool, remaining = sum([loads[i] for i in candidates]), spare
        for i in candidates:
            more = min(limit - counts[i], max(1, remaining * loads[i] // pool), spare)
            counts[i] = counts[i] + more
            spare = spare - more
    return np.array([limit] + counts)


def ragged(rng, amount, total, limit, skew):
    if amount == 2:
        one = jax.random.randint(rng, (), max(1, total - limit), min(limit, total - 1) + 1)
        return jnp.stack([one, total - one])
    tallies = jnp.asarray(split_up(amount, total, limit, skew), jnp.int32)
    couples = (amount - 1) // 2
    giver, taker = tallies[1:1 + 2 * couples:2], tallies[2:2 + 2 * couples:2]
    margin = jnp.minimum(giver - 1, limit - taker)
    moved = jax.random.randint(jax.random.fold_in(rng, 1), (couples,), 0, 1 << 20) % (margin + 1)
    tallies = tallies.at[1:1 + 2 * couples:2].set(giver - moved).at[2:2 + 2 * couples:2].set(taker + moved)
    return tallies[jax.random.permutation(jax.random.fold_in(rng, 2), amount)]


def normal_values(key, dims, scale, reach, held_as=jnp.bfloat16):
    values = scale * jax.random.normal(key, dims, jnp.float32)
    return jnp.clip(values, min=-reach, max=reach).astype(held_as)


def setup_inputs(seed: int = 0) -> dict:
    streams_of = jax.random.split(jax.random.key(seed), 7)
    contrast = jnp.clip(jax.random.uniform(streams_of[0], (2, NZ, NX, HEIGHT), jnp.float32, -0.15, 0.15) * block_levels(streams_of[0], (2, NZ, NX, HEIGHT), ((1, 4), (2, 8)), -0.4, 0.0), -0.15, 0.15)
    probe = normal_values(streams_of[1], (2, PATCH, PATCH), 1.0, 6.0, jnp.float32)
    offset_x = with_ends(jax.random.randint(streams_of[2], (PROBES,), 0, TILE), jax.random.fold_in(streams_of[2], 1), 0, TILE - 1).astype(jnp.int32)
    offset_y = with_ends(jax.random.randint(streams_of[3], (PROBES,), 0, HEIGHT - PATCH + 1), jax.random.fold_in(streams_of[3], 1), 0, HEIGHT - PATCH).astype(jnp.int32)
    probe_count = ragged(streams_of[4], N_LAT, 3 * N_LAT * SLOTS // 4, SLOTS, 1).astype(jnp.int32)
    measured = jnp.clip(4.0 * jax.random.uniform(streams_of[5], (PROBES, PATCH, PATCH), jnp.float32) ** block_levels(streams_of[5], (PROBES, PATCH, PATCH), ((0, 8),), -0.2, 0.2), 0.0, 4.0)
    return {"contrast": contrast, "probe": probe, "offset_x": offset_x, "offset_y": offset_y, "probe_count": probe_count, "measured": measured}


def tables(order):
    index = jnp.arange(order, dtype=jnp.int32)
    product = index[:, None] * index[None, :] % order
    theta = product.astype(jnp.float32) * (2.0 * math.pi / order)
    factor = 1.0 / math.sqrt(order)
    shifted = (index + order // 2) % order - order // 2
    quad = (shifted[:, None] * shifted[:, None] + shifted[None, :] * shifted[None, :]) % (4 * order)
    phase = quad.astype(jnp.float32) * (-math.pi / (2 * order))
    return (jnp.cos(theta) * factor, -jnp.sin(theta) * factor, jnp.cos(phase), jnp.sin(phase))

def left_product(matrix, field):
    return jnp.einsum('mn,...nk->...mk', matrix, field, precision=lax.Precision.HIGHEST)

def right_product(field, matrix):
    return jnp.einsum('...mn,nk->...mk', field, matrix, precision=lax.Precision.HIGHEST)

def both_sides(field_re, field_im, matrix_re, matrix_im):
    half_re = left_product(matrix_re, field_re) - left_product(matrix_im, field_im)
    half_im = left_product(matrix_re, field_im) + left_product(matrix_im, field_re)
    full_re = right_product(half_re, matrix_re) - right_product(half_im, matrix_im)
    full_im = right_product(half_re, matrix_im) + right_product(half_im, matrix_re)
    return (full_re, full_im)

def propagate(field_re, field_im, tabs, sign):
    dft_re, dft_im, kernel_re, kernel_im = tabs
    spec_re, spec_im = both_sides(field_re, field_im, dft_re, dft_im)
    signed_im = sign * kernel_im
    mixed_re = spec_re * kernel_re - spec_im * signed_im
    mixed_im = spec_re * signed_im + spec_im * kernel_re
    return both_sides(mixed_re, mixed_im, dft_re, -dft_im)

def far_field(exit_re, exit_im, observed, live, tabs):
    dft_re, dft_im = (tabs[0], tabs[1])
    far_re, far_im = both_sides(exit_re, exit_im, dft_re, dft_im)
    misfit = live[:, None, None] * (far_re * far_re + far_im * far_im - observed)
    return both_sides(misfit * far_re, misfit * far_im, dft_re, -dft_im)

def passed(field):
    return lax.optimization_barrier(field.astype(jnp.bfloat16)).astype(jnp.float32)

def reference(contrast, probe, offset_x, offset_y, probe_count, measured):
    tabs = tables(PATCH)
    padded = jnp.pad(contrast, ((0, 0), (0, 0), (0, PATCH), (0, 0)))
    anchor = jnp.zeros((), jnp.int32)
    groups = jnp.arange(N_BEAM, dtype=jnp.int32)

    def visit(accumulated, lat_item):
        lat_index, corner_x, corner_y, observed = lat_item
        corner_x = corner_x + lat_index * TILE

        def cut_block(x_start, y_start):
            return lax.dynamic_slice(padded, (anchor, anchor, x_start, y_start), (2, NZ, PATCH, PATCH))
        patches = jax.vmap(cut_block)(corner_x, corner_y)
        trans_re = (1.0 + jnp.transpose(patches[:, 0], (1, 0, 2, 3))).reshape(N_BEAM, SLICES, SLOTS, PATCH, PATCH)
        trans_im = jnp.transpose(patches[:, 1], (1, 0, 2, 3)).reshape(N_BEAM, SLICES, SLOTS, PATCH, PATCH)
        live = (jnp.arange(SLOTS, dtype=jnp.int32) < probe_count[lat_index]).astype(jnp.float32)
        start_re = jnp.broadcast_to(probe[0], (SLOTS, PATCH, PATCH))
        start_im = jnp.broadcast_to(probe[1], (SLOTS, PATCH, PATCH))

        def group_forward(wave, group_item):
            group_index, group_re, group_im = group_item
            wave_re, wave_im = wave
            kept_re = []
            kept_im = []
            for layer_index in range(SLICES):
                kept_re.append(wave_re)
                kept_im.append(wave_im)
                mult_re = group_re[layer_index] * wave_re - group_im[layer_index] * wave_im
                mult_im = group_re[layer_index] * wave_im + group_im[layer_index] * wave_re
                wave_re, wave_im = propagate(mult_re, mult_im, tabs, 1.0)
            final = group_index == N_BEAM - 1
            wave_re = jnp.where(final, wave_re, passed(wave_re))
            wave_im = jnp.where(final, wave_im, passed(wave_im))
            return ((wave_re, wave_im), (jnp.stack(kept_re), jnp.stack(kept_im)))
        exits, kept = lax.scan(group_forward, (start_re, start_im), (groups, trans_re, trans_im))
        adjoint = far_field(exits[0], exits[1], observed, live, tabs)

        def group_back(adjoint_now, group_item):
            group_index, group_re, group_im, saved_re, saved_im = group_item
            adj_re, adj_im = adjoint_now
            grads_re = [None] * SLICES
            grads_im = [None] * SLICES
            for layer_index in reversed(range(SLICES)):
                back_re, back_im = propagate(adj_re, adj_im, tabs, -1.0)
                psi_re = saved_re[layer_index]
                psi_im = saved_im[layer_index]
                grads_re[layer_index] = psi_re * back_re + psi_im * back_im
                grads_im[layer_index] = psi_re * back_im - psi_im * back_re
                adj_re, adj_im = (group_re[layer_index] * back_re + group_im[layer_index] * back_im, group_re[layer_index] * back_im - group_im[layer_index] * back_re)
            first_group = group_index == 0
            adj_re = jnp.where(first_group, adj_re, passed(adj_re))
            adj_im = jnp.where(first_group, adj_im, passed(adj_im))
            return ((adj_re, adj_im), (jnp.stack(grads_re), jnp.stack(grads_im)))
        unused, grads = lax.scan(group_back, adjoint, (groups, trans_re, trans_im, kept[0], kept[1]), reverse=True)
        grad_re = grads[0].reshape(NZ, SLOTS, PATCH, PATCH)
        grad_im = grads[1].reshape(NZ, SLOTS, PATCH, PATCH)
        for slot_index in range(SLOTS):
            piece = jnp.stack([grad_re[:, slot_index], grad_im[:, slot_index]])
            place = (anchor, anchor, corner_x[slot_index], corner_y[slot_index])
            current = lax.dynamic_slice(accumulated, place, piece.shape)
            accumulated = lax.dynamic_update_slice(accumulated, current + piece, place)
        return (accumulated, None)
    lat_items = (jnp.arange(N_LAT, dtype=jnp.int32), offset_x.reshape(N_LAT, SLOTS), offset_y.reshape(N_LAT, SLOTS), measured.reshape(N_LAT, SLOTS, PATCH, PATCH))
    accumulated, unused = lax.scan(visit, jnp.zeros(padded.shape, jnp.float32), lat_items)
    return accumulated[:, :, :NX]
```

```python
import functools
import math

import jax
import jax.numpy as jnp
import ml_dtypes
import numpy as np
from jax import lax
from jax.experimental import pallas as pl
from jax.experimental.pallas import tpu as pltpu
from jax.sharding import PartitionSpec as P

AXES = ("beam", "lat")


def matrices(order):
    index = np.arange(order)
    dft = np.exp(-2j * np.pi * (index[:, None] * index[None, :] % order) / order) / math.sqrt(order)
    freq = (index + order // 2) % order - order // 2
    phase = np.exp(-1j * np.pi * (freq * freq % (4 * order)) / (2 * order))
    prop = (dft.conj() * phase) @ dft
    parts = np.stack([prop.real, prop.imag, dft.real, dft.imag])
    high = parts.astype(ml_dtypes.bfloat16)
    low = (parts - high.astype(np.float64)).astype(ml_dtypes.bfloat16)
    return np.stack([high, low])


def place(n, lats, slice_index):
    first, second = n // 2 - 1, n // 2
    mirror = n - 1 - slice_index
    to = {slice_index: first, mirror: second}
    if slice_index not in (first, second):
        to[first] = min(slice_index, mirror)
        to[second] = max(slice_index, mirror)
    pairs = []
    for b in range(n):
        for l in range(lats):
            goal = to.get(b, b)
            if goal == second:
                spot = (goal, (l - 1) % lats)
            elif goal == b:
                spot = (goal, l ^ 1)
            else:
                spot = (goal, l)
            pairs.append((b * lats + l, spot[0] * lats + spot[1]))
    return pairs


def swap(n, lats):
    return [(b * lats + l, b * lats + (l ^ 1)) for b in range(n) for l in range(lats)]


def kernel(
    n, lats, slots, mine_ref, near_ref, mats_ref, own_ref, other_ref, probe_ref, meas_ref, near_meas_ref,
    keep_ref, send_ref, full_ref, trn_ref, psi_ref,
):
    order = probe_ref.shape[-1]
    tile = own_ref.shape[2]
    half = slots // 2
    first, second = n // 2 - 1, n // 2
    group = lax.axis_index("beam")
    lat = lax.axis_index("lat")
    side = lax.rem(lat, 2)
    at_first = group == first
    at_second = group == second
    base = jnp.where(at_first, lat - side, lat + 1 - side)
    local = base == lat
    beyond = base + 1 >= lats

    def scalar(i):
        return jnp.where(local, mine_ref[i], near_ref[i])

    slot_of = [side * half + s for s in range(half)]
    xs = [scalar(slot_of[s]) for s in range(half)]
    ys = [scalar(slots + slot_of[s]) for s in range(half)]
    count = scalar(2 * slots)

    for h in range(2):
        for m in range(2):
            re, im = mats_ref[h, 2 * m], mats_ref[h, 2 * m + 1]
            full_ref[h, 2 * m, :order, :order] = re
            full_ref[h, 2 * m, :order, order:] = -im
            full_ref[h, 2 * m, order:, :order] = im
            full_ref[h, 2 * m, order:, order:] = re
            full_ref[h, 2 * m + 1, :order, :order] = re
            full_ref[h, 2 * m + 1, :order, order:] = im
            full_ref[h, 2 * m + 1, order:, :order] = -im
            full_ref[h, 2 * m + 1, order:, order:] = re

    lane = lax.broadcasted_iota(jnp.int32, (order, order), 1)

    def stacked(k):
        return jnp.where(at_second, n - 1 - k, k)

    def column(axis, shape):
        index = lax.broadcasted_iota(jnp.int32, shape, axis)
        other_side = jnp.where(index >= tile, 1 - side, side)
        return jnp.where(index >= tile, index - tile, index) + other_side * tile

    wide, tall = (order, 2 * tile), (2 * tile, order)
    last = jnp.where(beyond, tile, 2 * tile)
    from_col = column(1, wide)
    cut_at = jnp.where(from_col < last, from_col - lax.broadcasted_iota(jnp.int32, wide, 0), -1)
    cuts = jnp.concatenate([jnp.where(cut_at == x, 1.0, 0.0) for x in xs], axis=0).astype(jnp.bfloat16)
    put_at = column(0, tall) - lax.broadcasted_iota(jnp.int32, tall, 1)
    puts = jnp.concatenate([jnp.where(put_at == x, 1.0, 0.0) for x in xs], axis=1).astype(jnp.bfloat16)

    def dot(a, b):
        return jnp.dot(a, b, preferred_element_type=jnp.float32)

    def cut(k, c):
        i = stacked(k)
        own, other = own_ref[i, c], other_ref[i, c]
        if k == first:
            own, other = jnp.where(at_first, other, own), jnp.where(at_first, own, other)
        blocks = dot(cuts, jnp.concatenate([own, other], axis=0))
        out = []
        for s in range(half):
            rows = slice(s * order, (s + 1) * order)
            turn = lax.rem(order - ys[s], order)
            left = pltpu.roll(blocks[rows, :order], turn, 1)
            right = pltpu.roll(blocks[rows, order:], turn, 1)
            out.append(jnp.where(lane < order - ys[s], left, right))
        return out

    def put(k, c, values):
        rows = []
        for s, value in enumerate(values):
            value = pltpu.roll(value, lax.rem(ys[s], order), 1)
            rows.append(
                jnp.concatenate(
                    [jnp.where(lane >= ys[s], value, 0.0), jnp.where(lane < ys[s], value, 0.0)], axis=1
                ).astype(jnp.bfloat16)
            )
        total = dot(puts, jnp.concatenate(rows, axis=0))
        i = stacked(k)
        keep_ref[i, c] = total[:tile]
        send_ref[i, c] = total[tile:].astype(jnp.bfloat16)

    def sandwich(pair, m, conj):
        right = 2 * m + (0 if conj else 1)
        left = 2 * m + (1 if conj else 0)
        rows = jnp.concatenate([jnp.concatenate(w, axis=1) for w in pair], axis=0).astype(jnp.bfloat16)
        y = dot(rows, full_ref[0, right]) + dot(rows, full_ref[1, right])
        y = y.astype(jnp.bfloat16)
        cols = jnp.concatenate(
            [
                jnp.concatenate([y[:order, :order], y[order:, :order]], axis=1),
                jnp.concatenate([y[:order, order:], y[order:, order:]], axis=1),
            ],
            axis=0,
        )
        z = dot(full_ref[0, left], cols) + dot(full_ref[1, left], cols)
        return [(z[:order, :order], z[order:, :order]), (z[:order, order:], z[order:, order:])]

    pairs = [(s, s + 1) for s in range(0, half, 2)]
    waves = [[(probe_ref[0], probe_ref[1])] * 2 for _ in pairs]
    for k in range(n):
        cut_re, cut_im = cut(k, 0), cut(k, 1)
        for j, pair in enumerate(pairs):
            mult = []
            for q, s in enumerate(pair):
                re, im = waves[j][q]
                psi_ref[k, s, 0] = re
                psi_ref[k, s, 1] = im
                t_re, t_im = 1.0 + cut_re[s], cut_im[s]
                trn_ref[k, s, 0] = t_re
                trn_ref[k, s, 1] = t_im
                mult.append((t_re * re - t_im * im, t_re * im + t_im * re))
            waves[j] = sandwich(mult, 0 if k < n - 1 else 1, False)

    back = [None] * len(pairs)
    for j, pair in enumerate(pairs):
        scaled = []
        for q, s in enumerate(pair):
            re, im = waves[j][q]
            slot = slot_of[s]
            seen = jnp.where(local, meas_ref[slot], near_meas_ref[slot])
            misfit = jnp.where(slot < count, re * re + im * im - seen, 0.0)
            scaled.append((misfit * re, misfit * im))
        back[j] = sandwich(scaled, 1, True)
    for k in reversed(range(n)):
        grad_re, grad_im = [], []
        for j, pair in enumerate(pairs):
            mult = []
            for q, s in enumerate(pair):
                re, im = back[j][q]
                p_re, p_im = psi_ref[k, s, 0], psi_ref[k, s, 1]
                grad_re.append(p_re * re + p_im * im)
                grad_im.append(p_re * im - p_im * re)
                if k > 0:
                    t_re, t_im = trn_ref[k, s, 0], trn_ref[k, s, 1]
                    mult.append((t_re * re + t_im * im, t_re * im - t_im * re))
            if k > 0:
                back[j] = sandwich(mult, 0, True)
        put(k, 0, grad_re)
        put(k, 1, grad_im)


def on_device(contrast, probe, offset_x, offset_y, probe_count, measured):
    n, lats = lax.axis_size("beam"), lax.axis_size("lat")
    order, tile, height = probe.shape[1], contrast.shape[2], contrast.shape[3]
    slots = offset_x.shape[0]
    half = slots // 2
    first, second = n // 2 - 1, n // 2
    lat, group = lax.axis_index("lat"), lax.axis_index("beam")
    routes = [place(n, lats, a) for a in range(n)]
    turn = sorted(range(n), key=lambda a: (a in (first, second), a in (second,), a))
    partner = swap(n, lats)

    mine = jnp.concatenate([offset_x, offset_y, probe_count])
    near = lax.ppermute(mine, AXES, partner)
    near_measured = lax.ppermute(measured, AXES, partner)
    own_tile = contrast[:, 0].astype(jnp.bfloat16)[None]
    arrived = {a: lax.ppermute(own_tile, AXES, routes[a]) for a in turn}
    own = jnp.concatenate([arrived[a] for a in range(n)], axis=0)
    other = lax.ppermute(own, AXES, partner)

    smem = pl.BlockSpec(memory_space=pltpu.SMEM)
    vmem = pl.BlockSpec(memory_space=pltpu.VMEM)
    mats = jnp.asarray(matrices(order))
    tiles = (n, 2, tile, height)
    keep, send = pl.pallas_call(
        functools.partial(kernel, n, lats, slots),
        out_shape=(jax.ShapeDtypeStruct(tiles, jnp.float32), jax.ShapeDtypeStruct(tiles, jnp.bfloat16)),
        in_specs=[smem, smem] + [vmem] * 6,
        out_specs=(vmem, vmem),
        scratch_shapes=[
            pltpu.VMEM((2, 4, 2 * order, 2 * order), jnp.bfloat16),
            pltpu.VMEM((n, half, 2, order, order), jnp.float32),
            pltpu.VMEM((n, half, 2, order, order), jnp.float32),
        ],
        compiler_params=pltpu.CompilerParams(vmem_limit_bytes=(16 + 2 * n) << 20),
    )(mine, near, mats, own, other, probe, measured, near_measured)

    from_partner = lax.ppermute(send, AXES, partner)
    totals = [(keep[i] + from_partner[i].astype(jnp.float32)).astype(jnp.bfloat16) for i in range(n)]
    returned = {a: lax.ppermute(totals[a], AXES, [(d, s) for s, d in routes[a]]) for a in turn}
    from_first = totals[first]
    from_second = returned[n - 1]
    for g in range(n):
        if g != first:
            from_first = jnp.where(group == g, returned[g], from_first)
        from_second = jnp.where(group == g, returned[n - 1 - g], from_second)
    from_second = jnp.where(lat == 0, 0.0, from_second.astype(jnp.float32))
    return (from_first.astype(jnp.float32) + from_second)[:, None]


def solution(mesh):
    in_specs = (
        P(None, "beam", "lat", None),
        P(),
        P("lat"),
        P("lat"),
        P("lat"),
        P("lat", None, None),
    )
    out_specs = P(None, "beam", "lat", None)
    return jax.shard_map(
        on_device, mesh=mesh, in_specs=in_specs, out_specs=out_specs, check_vma=False
    )
```

```python
import functools
import math

import jax
import jax.numpy as jnp
import ml_dtypes
import numpy as np
from jax import lax
from jax.experimental import pallas as pl
from jax.experimental.pallas import tpu as pltpu
from jax.sharding import PartitionSpec as P

AXES = ("beam", "lat")


W_SCALE = 1.1775


def matrices(order, steps):
    index = np.arange(order)
    dft = np.exp(-2j * np.pi * (index[:, None] * index[None, :] % order) / order) / math.sqrt(order)
    freq = (index + order // 2) % order - order // 2
    phase = np.exp(-1j * np.pi * (freq * freq % (4 * order)) / (2 * order))
    prop = (dft.conj() * phase) @ dft

    def pair(matrix):
        return np.stack([matrix.real, matrix.imag]).astype(ml_dtypes.bfloat16)

    def value(parts):
        parts = parts.astype(np.float64)
        return parts[0] + 1j * parts[1]

    out, ahead = [], np.zeros_like(prop)
    for step in range(steps):
        out.append(pair(prop - ahead))
        if step == steps - 1:
            out.append(pair(prop - ahead - value(out[-1])))
        else:
            ahead = ahead + value(out[-1]) - prop
    out.append(pair(W_SCALE * dft))
    return np.stack(out)


def place(n, lats, slice_index, short):
    first, second = n // 2 - 1, n // 2
    mirror = n - 1 - slice_index
    goals = {slice_index: first, mirror: second}
    outer = slice_index not in (first, second)
    if outer:
        goals[first] = min(slice_index, mirror)
        goals[second] = max(slice_index, mirror)
    to = {}
    for b in range(n):
        for l in range(lats):
            goal = goals.get(b, b)
            if goal == second:
                to[b, l] = (goal, (l - 1) % lats)
            else:
                to[b, l] = (goal, l ^ 1 if goal == b else l)
    if outer and short:
        via, middle = (first if goals[first] == mirror else second), lats // 4
        to[mirror, 0] = (mirror, middle)
        to[via, middle] = (second, lats - 1)
    return [(b * lats + l, c * lats + m) for (b, l), (c, m) in to.items()]


def swap(n, lats):
    return [(b * lats + l, b * lats + (l ^ 1)) for b in range(n) for l in range(lats)]


def turns(n, back):
    ends = [0, n - 1] if back else [n - 1, 0]
    return ends + list(range(1, n - 1))


def kernel(
    n, lats, slots, mine_ref, near_ref, mats_ref, own_ref, other_ref, probe_ref, meas_ref, near_meas_ref,
    keep_ref, send_ref, full_ref, trn_ref, psi_ref, ext_ref,
):
    order = probe_ref.shape[-1]
    tile = own_ref.shape[2]
    half = slots // 2
    first, second = n // 2 - 1, n // 2
    group = lax.axis_index("beam")
    lat = lax.axis_index("lat")
    side = lax.rem(lat, 2)
    at_first = group == first
    at_second = group == second
    base = jnp.where(at_first, lat - side, lat + 1 - side)
    local = base == lat
    beyond = base + 1 >= lats

    def scalar(i):
        return jnp.where(local, mine_ref[i], near_ref[i])

    slot_of = [side * half + s for s in range(half)]
    xs = [scalar(slot_of[s]) for s in range(half)]
    ys = [scalar(slots + slot_of[s]) for s in range(half)]
    count = scalar(2 * slots)

    for m in range(n + 1):
        re, im = mats_ref[m, 0], mats_ref[m, 1]
        for h, (upper, lower) in enumerate(((-im, im), (im, -im))):
            full_ref[m, h, :order, :order] = re
            full_ref[m, h, :order, order:] = upper
            full_ref[m, h, order:, :order] = lower
            full_ref[m, h, order:, order:] = re

    lane = lax.broadcasted_iota(jnp.int32, (order, order), 1)

    def spot(k, back):
        order = turns(n, back)
        return jnp.where(at_second, order.index(n - 1 - k), order.index(k))

    def column(axis, shape):
        index = lax.broadcasted_iota(jnp.int32, shape, axis)
        other_side = jnp.where(index >= tile, 1 - side, side)
        return jnp.where(index >= tile, index - tile, index) + other_side * tile

    tall = (2 * tile, order)
    put_at = column(0, tall) - lax.broadcasted_iota(jnp.int32, tall, 1)
    puts = jnp.concatenate([jnp.where(put_at == x, 1.0, 0.0) for x in xs], axis=1).astype(jnp.bfloat16)

    def dot(a, b):
        return jnp.dot(a, b, preferred_element_type=jnp.float32)

    for k in range(n):
        i = spot(k, False)
        row = jnp.where(at_first & (k == first), 1 - side, side)
        for ref, r in ((own_ref, row), (other_ref, 1 - row)):
            value = ref[i].astype(jnp.float32) * jnp.where(beyond & (r == 1), 0.0, 1.0)
            ext_ref[k, :, pl.ds(pl.multiple_of(r * tile, tile), tile), :] = value

    sub = lax.broadcasted_iota(jnp.int32, (order // 8, 8, order), 1)
    longer = lax.broadcasted_iota(jnp.int32, (order + 8, order), 1)

    def cut(k, c):
        out = []
        for s in range(half):
            turn = lax.rem(order - ys[s], order)
            start = pl.ds(pl.multiple_of(xs[s] // 8 * 8, 8), order + 8)
            left = pltpu.roll(ext_ref[k, c, start, :order], turn, 1)
            right = pltpu.roll(ext_ref[k, c, start, order:], turn, 1)
            w = jnp.where(longer < order - ys[s], left, right).reshape(order // 8 + 1, 8, order)
            r = lax.rem(xs[s], 8)
            w = pltpu.roll(w, lax.rem(8 - r, 8), 1)
            out.append(jnp.where(sub < 8 - r, w[:-1], w[1:]).reshape(order, order))
        return out

    def put(k, c, values):
        rows = []
        for s, value in enumerate(values):
            value = pltpu.roll(value, lax.rem(ys[s], order), 1)
            rows.append(
                jnp.concatenate(
                    [jnp.where(lane >= ys[s], value, 0.0), jnp.where(lane < ys[s], value, 0.0)], axis=1
                ).astype(jnp.bfloat16)
            )
        total = dot(puts, jnp.concatenate(rows, axis=0))
        i = spot(k, True)
        keep_ref[i, c] = total[:tile]
        send_ref[i, c] = total[tile:].astype(jnp.bfloat16)

    def sandwich(pairs, ms, conj):
        right, left = (0, 1) if conj else (1, 0)
        rows = [jnp.concatenate([jnp.concatenate(w, axis=1) for w in p], axis=0).astype(jnp.bfloat16) for p in pairs]
        ys = [sum(dot(r, full_ref[m, right]) for m in ms).astype(jnp.bfloat16) for r in rows]
        cols = [
            jnp.concatenate(
                [
                    jnp.concatenate([y[q * order : (q + 1) * order, c * order : (c + 1) * order] for q in range(1)], axis=1)
                    for c in range(2)
                ],
                axis=0,
            )
            for y in ys
        ]
        zs = [sum(dot(full_ref[m, left], c) for m in ms) for c in cols]
        return [[(z[:order, q * order : (q + 1) * order], z[order:, q * order : (q + 1) * order]) for q in range(1)] for z in zs]

    def step(i):
        return (n - 2, n - 1) if i == n - 2 else (i,)

    transform = (n,)
    pairs = [tuple(range(s, s + 1)) for s in range(0, half, 1)]
    waves = [[(probe_ref[0], probe_ref[1])] * 1 for _ in pairs]
    for k in range(n):
        cut_re, cut_im = cut(k, 0), cut(k, 1)
        mults = []
        for j, pair in enumerate(pairs):
            mult = []
            for q, s in enumerate(pair):
                re, im = waves[j][q]
                psi_ref[k, s, 0] = re
                psi_ref[k, s, 1] = im
                t_re, t_im = 1.0 + cut_re[s], cut_im[s]
                trn_ref[k, s, 0] = t_re
                trn_ref[k, s, 1] = t_im
                mult.append((t_re * re - t_im * im, t_re * im + t_im * re))
            mults.append(mult)
        waves = sandwich(mults, step(k) if k < n - 1 else transform, False)

    mults = []
    for j, pair in enumerate(pairs):
        scaled = []
        for q, s in enumerate(pair):
            re, im = waves[j][q]
            slot = slot_of[s]
            seen = jnp.where(local, meas_ref[slot], near_meas_ref[slot])
            misfit = jnp.where(slot < count, (re * re + im * im) * W_SCALE**-8 - seen * W_SCALE**-4, 0.0)
            scaled.append((misfit * re, misfit * im))
        mults.append(scaled)
    back = sandwich(mults, transform, True)
    for k in reversed(range(n)):
        grad_re, grad_im, mults = [], [], []
        for j, pair in enumerate(pairs):
            mult = []
            for q, s in enumerate(pair):
                re, im = back[j][q]
                p_re, p_im = psi_ref[k, s, 0], psi_ref[k, s, 1]
                grad_re.append(p_re * re + p_im * im)
                grad_im.append(p_re * im - p_im * re)
                if k > 0:
                    t_re, t_im = trn_ref[k, s, 0], trn_ref[k, s, 1]
                    mult.append((t_re * re + t_im * im, t_re * im - t_im * re))
            mults.append(mult)
        if k > 0:
            back = sandwich(mults, step(n - 1 - k), True)
        put(k, 0, grad_re)
        put(k, 1, grad_im)


def on_device(contrast, probe, offset_x, offset_y, probe_count, measured):
    n, lats = lax.axis_size("beam"), lax.axis_size("lat")
    order, tile, height = probe.shape[1], contrast.shape[2], contrast.shape[3]
    slots = offset_x.shape[0]
    half = slots // 2
    first = n // 2 - 1
    lat, group = lax.axis_index("lat"), lax.axis_index("beam")
    routes = [place(n, lats, a, False) for a in range(n)]
    back_routes = [place(n, lats, a, True) for a in range(n)]
    turn, back_turn = turns(n, False), turns(n, True)
    partner = swap(n, lats)

    mine = jnp.concatenate([offset_x, offset_y, probe_count])
    own_tile = contrast[:, 0].astype(jnp.bfloat16)[None]
    near = lax.ppermute(mine, AXES, partner)
    near_measured = lax.ppermute(measured, AXES, partner)
    own = jnp.concatenate([lax.ppermute(own_tile, AXES, routes[a]) for a in turn], axis=0)
    own, near, near_measured = lax.optimization_barrier((own, near, near_measured))
    other = lax.ppermute(own, AXES, partner)

    smem = pl.BlockSpec(memory_space=pltpu.SMEM)
    vmem = pl.BlockSpec(memory_space=pltpu.VMEM)
    mats = jnp.asarray(matrices(order, n - 1))
    tiles = (n, 2, tile, height)
    keep, send = pl.pallas_call(
        functools.partial(kernel, n, lats, slots),
        out_shape=(jax.ShapeDtypeStruct(tiles, jnp.float32), jax.ShapeDtypeStruct(tiles, jnp.bfloat16)),
        in_specs=[smem, smem] + [vmem] * 6,
        out_specs=(vmem, vmem),
        scratch_shapes=[
            pltpu.VMEM((n + 1, 2, 2 * order, 2 * order), jnp.bfloat16),
            pltpu.VMEM((n, half, 2, order, order), jnp.float32),
            pltpu.VMEM((n, half, 2, order, order), jnp.float32),
            pltpu.VMEM((n, 2, 2 * tile, height), jnp.float32),
        ],
        compiler_params=pltpu.CompilerParams(vmem_limit_bytes=(16 + 3 * n) << 20),
    )(mine, near, mats, own, other, probe, measured, near_measured)

    from_partner = lax.ppermute(send, AXES, partner)
    totals = [(keep[i] + from_partner[i].astype(jnp.float32)).astype(jnp.bfloat16) for i in range(n)]
    returned = [lax.ppermute(totals[i], AXES, [(d, s) for s, d in back_routes[a]]) for i, a in enumerate(back_turn)]
    returned = jnp.concatenate([r[None] for r in returned], axis=0)
    spot_first, spot_second = jnp.int32(0), jnp.int32(0)
    for i, a in enumerate(back_turn):
        spot_first = jnp.where(group == a, i, spot_first)
        spot_second = jnp.where(group == n - 1 - a, i, spot_second)
    from_first = lax.dynamic_index_in_dim(returned, spot_first, 0, False)
    from_first = jnp.where(group == first, totals[back_turn.index(first)], from_first)
    from_second = lax.dynamic_index_in_dim(returned, spot_second, 0, False).astype(jnp.float32)
    from_second = jnp.where(lat == 0, 0.0, from_second)
    return (from_first.astype(jnp.float32) + from_second)[:, None]


def solution(mesh):
    in_specs = (
        P(None, "beam", "lat", None),
        P(),
        P("lat"),
        P("lat"),
        P("lat"),
        P("lat", None, None),
    )
    out_specs = P(None, "beam", "lat", None)
    return jax.shard_map(
        on_device, mesh=mesh, in_specs=in_specs, out_specs=out_specs, check_vma=False
    )
```

```python
import functools
import math

import jax
import jax.numpy as jnp
import ml_dtypes
import numpy as np
from jax import lax
from jax.experimental import pallas as pl
from jax.experimental.pallas import tpu as pltpu
from jax.sharding import PartitionSpec as P

AXES = ("beam", "lat")


W_SCALE = 1.1775
LANES = 128


def matrices(order, steps):
    index = np.arange(order)
    dft = np.exp(-2j * np.pi * (index[:, None] * index[None, :] % order) / order) / math.sqrt(order)
    freq = (index + order // 2) % order - order // 2
    phase = np.exp(-1j * np.pi * (freq * freq % (4 * order)) / (2 * order))
    prop = (dft.conj() * phase) @ dft

    def pair(matrix):
        return np.stack([matrix.real, matrix.imag]).astype(ml_dtypes.bfloat16)

    def value(parts):
        parts = parts.astype(np.float64)
        return parts[0] + 1j * parts[1]

    out, ahead = [], np.zeros_like(prop)
    for step in range(steps):
        out.append(pair(prop - ahead))
        if step == steps - 1:
            out.append(pair(prop - ahead - value(out[-1])))
        else:
            ahead = ahead + value(out[-1]) - prop
    out.append(pair(W_SCALE * dft))
    return np.stack(out)


def place(n, lats, slice_index, short):
    first, second = n // 2 - 1, n // 2
    mirror = n - 1 - slice_index
    goals = {slice_index: first, mirror: second}
    outer = slice_index not in (first, second)
    if outer:
        goals[first] = min(slice_index, mirror)
        goals[second] = max(slice_index, mirror)
    to = {}
    for b in range(n):
        for l in range(lats):
            goal = goals.get(b, b)
            if goal == second:
                to[b, l] = (goal, (l - 1) % lats)
            else:
                to[b, l] = (goal, l ^ 1 if goal == b else l)
    if outer and short:
        via, middle = (first if goals[first] == mirror else second), lats // 4
        to[mirror, 0] = (mirror, middle)
        to[via, middle] = (second, lats - 1)
    return [(b * lats + l, c * lats + m) for (b, l), (c, m) in to.items()]


def swap(n, lats):
    return [(b * lats + l, b * lats + (l ^ 1)) for b in range(n) for l in range(lats)]


def turns(n, back):
    ends = [0, n - 1] if back else [n - 1, 0]
    return ends + list(range(1, n - 1))


def position(n, lats):
    group, lat = lax.axis_index("beam"), lax.axis_index("lat")
    side = lax.rem(lat, 2)
    at_first, at_second = group == n // 2 - 1, group == n // 2
    base = jnp.where(at_first, lat - side, lat + 1 - side)
    return lat, side, at_first, at_second, base


def corners(slots, local, side, mine_ref, near_ref):
    half = slots // 2
    values = jnp.where(local, mine_ref[...], near_ref[...])

    def scalar(i):
        return jnp.where(side == 0, values[0, i], values[0, i + half])

    return [scalar(s) for s in range(half)], [scalar(slots + s) for s in range(half)], values[0, 2 * slots]


def lay(ext_ref, k, own, other, row, beyond, tile):
    for value, r in ((own, row), (other, 1 - row)):
        value = value.astype(jnp.float32) * jnp.where(beyond & (r == 1), 0.0, 1.0)
        ext_ref[k, :, pl.ds(pl.multiple_of(r * tile, tile), tile), :] = value


def cut(ext_ref, k, c, xs, ys, order):
    sub = lax.broadcasted_iota(jnp.int32, (order // 8, 8, order), 1)
    lane = lax.broadcasted_iota(jnp.int32, (order + 8, order), 1)
    out = []
    for x, y in zip(xs, ys):
        turn = lax.rem(order - y, order)
        start = pl.ds(pl.multiple_of(x // 8 * 8, 8), order + 8)
        left = pltpu.roll(ext_ref[k, c, start, :order], turn, 1)
        right = pltpu.roll(ext_ref[k, c, start, order:], turn, 1)
        w = jnp.where(lane < order - y, left, right).reshape(order // 8 + 1, 8, order)
        r = lax.rem(x, 8)
        w = pltpu.roll(w, lax.rem(8 - r, 8), 1)
        out.append(jnp.where(sub < 8 - r, w[:-1], w[1:]).reshape(order, order))
    return out


def dot(a, b):
    return jnp.dot(a, b, preferred_element_type=jnp.float32)


def sandwich(full_ref, waves, ms, conj):
    order = waves[0][0].shape[0]
    right, left = (0, 1) if conj else (1, 0)
    rows = [jnp.concatenate(w, axis=1).astype(jnp.bfloat16) for w in waves]
    ys = [sum(dot(r, full_ref[m, right]) for m in ms).astype(jnp.bfloat16) for r in rows]
    cols = [jnp.concatenate([y[:, :order], y[:, order:]], axis=0) for y in ys]
    zs = [sum(dot(full_ref[m, left], c) for m in ms) for c in cols]
    return [(z[:order], z[order:]) for z in zs]


def step(n, i):
    return (n - 2, n - 1) if i == n - 2 else (i,)


def early_kernel(
    n, lats, slots, mine_ref, near_ref, mats_ref, own_ref, other_ref, probe_ref, full_ref, psi_ref, trn_ref, ext_ref
):
    order, tile = probe_ref.shape[-1], own_ref.shape[2]
    lat, side, at_first, at_second, base = position(n, lats)
    xs, ys, count = corners(slots, base == lat, side, mine_ref, near_ref)
    for m in range(n + 1):
        re, im = mats_ref[m, 0], mats_ref[m, 1]
        for h, (upper, lower) in enumerate(((-im, im), (im, -im))):
            full_ref[m, h, :order, :order] = re
            full_ref[m, h, :order, order:] = upper
            full_ref[m, h, order:, :order] = lower
            full_ref[m, h, order:, order:] = re
    for k in range(2):
        i = jnp.where(at_second, k, 1 - k)
        lay(ext_ref, k, own_ref[i], other_ref[i], side, base + 1 >= lats, tile)
    first = [cut(ext_ref, 0, c, xs, ys, order) for c in range(2)]
    re, im = probe_ref[0], probe_ref[1]
    waves = []
    for c_re, c_im in zip(*first):
        t_re = 1.0 + c_re
        waves.append((t_re * re - c_im * im, t_re * im + c_im * re))
    waves = sandwich(full_ref, waves, step(n, 0), False)
    for s, wave in enumerate(waves):
        for c in range(2):
            psi_ref[s, c] = wave[c]
    for c in range(2):
        for s, value in enumerate(cut(ext_ref, 1, c, xs, ys, order)):
            trn_ref[s, c] = value


def main_kernel(
    n, lats, slots, mine_ref, near_ref, full_ref, own_ref, other_ref, probe_ref, one_ref, last_ref, meas_ref,
    near_meas_ref, keep_ref, send_ref, trn_ref, psi_ref, ext_ref,
):
    order, tile = probe_ref.shape[-1], own_ref.shape[2]
    half = slots // 2
    first = n // 2 - 1
    lat, side, at_first, at_second, base = position(n, lats)
    local = base == lat
    xs, ys, count = corners(slots, local, side, mine_ref, near_ref)
    lane = lax.broadcasted_iota(jnp.int32, (order, order), 1)

    tall = (2 * tile, order)
    index = lax.broadcasted_iota(jnp.int32, tall, 0)
    column = jnp.where(index >= tile, index - tile + (1 - side) * tile, index + side * tile)
    put_at = column - lax.broadcasted_iota(jnp.int32, tall, 1)
    puts = jnp.concatenate([jnp.where(put_at == x, 1.0, 0.0) for x in xs], axis=1).astype(jnp.bfloat16)

    def put(k, c, values):
        rows = []
        for s, value in enumerate(values):
            value = pltpu.roll(value, lax.rem(ys[s], order), 1)
            rows.append(
                jnp.concatenate(
                    [jnp.where(lane >= ys[s], value, 0.0), jnp.where(lane < ys[s], value, 0.0)], axis=1
                ).astype(jnp.bfloat16)
            )
        total = dot(puts, jnp.concatenate(rows, axis=0))
        order_back = turns(n, True)
        i = jnp.where(at_second, order_back.index(n - 1 - k), order_back.index(k))
        keep_ref[i, c] = total[:tile]
        send_ref[i, c] = total[tile:].astype(jnp.bfloat16)

    for k in range(1, n - 1):
        i = jnp.where(at_second, n - 2 - k, k - 1)
        row = jnp.where(at_first & (k == first), 1 - side, side)
        lay(ext_ref, k - 1, own_ref[i], other_ref[i], row, base + 1 >= lats, tile)

    waves = [(one_ref[s, 0], one_ref[s, 1]) for s in range(half)]
    for k in range(1, n):
        if k < n - 1:
            cuts = [cut(ext_ref, k - 1, c, xs, ys, order) for c in range(2)]
        else:
            cuts = [[last_ref[s, c] for s in range(half)] for c in range(2)]
        mult = []
        for s, (re, im) in enumerate(waves):
            psi_ref[k, s, 0] = re
            psi_ref[k, s, 1] = im
            t_re, t_im = 1.0 + cuts[0][s], cuts[1][s]
            trn_ref[k, s, 0] = t_re
            trn_ref[k, s, 1] = t_im
            mult.append((t_re * re - t_im * im, t_re * im + t_im * re))
        waves = sandwich(full_ref, mult, step(n, k) if k < n - 1 else (n,), False)

    mult = []
    for s, (re, im) in enumerate(waves):
        slot = side * half + s
        seen = jnp.where(local, meas_ref[slot], near_meas_ref[slot])
        misfit = jnp.where(slot < count, (re * re + im * im) * W_SCALE**-8 - seen * W_SCALE**-4, 0.0)
        mult.append((misfit * re, misfit * im))
    waves = sandwich(full_ref, mult, (n,), True)
    for k in reversed(range(n)):
        grad_re, grad_im, mult = [], [], []
        for s, (re, im) in enumerate(waves):
            p_re, p_im = (psi_ref[k, s, 0], psi_ref[k, s, 1]) if k else (probe_ref[0], probe_ref[1])
            grad_re.append(p_re * re + p_im * im)
            grad_im.append(p_re * im - p_im * re)
            if k > 0:
                t_re, t_im = trn_ref[k, s, 0], trn_ref[k, s, 1]
                mult.append((t_re * re + t_im * im, t_re * im - t_im * re))
        if k > 0:
            waves = sandwich(full_ref, mult, step(n, n - 1 - k), True)
        put(k, 0, grad_re)
        put(k, 1, grad_im)


def on_device(contrast, probe, offset_x, offset_y, probe_count, measured):
    n, lats = lax.axis_size("beam"), lax.axis_size("lat")
    order, tile, height = probe.shape[1], contrast.shape[2], contrast.shape[3]
    slots = offset_x.shape[0]
    half = slots // 2
    first = n // 2 - 1
    lat, group = lax.axis_index("lat"), lax.axis_index("beam")
    routes = [place(n, lats, a, False) for a in range(n)]
    back_routes = [place(n, lats, a, True) for a in range(n)]
    turn, back_turn = turns(n, False), turns(n, True)
    partner = swap(n, lats)

    own_tile = contrast[:, 0].astype(jnp.bfloat16)[None]
    arrived = [lax.ppermute(own_tile, AXES, routes[a]) for a in turn]
    own_early = jnp.concatenate(arrived[:2], axis=0)
    own_late = jnp.concatenate(arrived[2:], axis=0)
    mine = jnp.concatenate([offset_x, offset_y, probe_count])
    mine = jnp.pad(mine, (0, LANES - mine.shape[0]))[None]
    near = lax.ppermute(mine, AXES, partner)
    near_measured = lax.ppermute(measured, AXES, partner)
    own_early, near = lax.optimization_barrier((own_early, near))
    other_early = lax.ppermute(own_early, AXES, partner)
    other_late = lax.ppermute(own_late, AXES, partner)

    vmem = pl.BlockSpec(memory_space=pltpu.VMEM)
    params = pltpu.CompilerParams(vmem_limit_bytes=(16 + 3 * n) << 20)
    mats = jnp.asarray(matrices(order, n - 1))
    tiles = (n, 2, tile, height)
    fields = jax.ShapeDtypeStruct((half, 2, order, order), jnp.float32)
    full = jax.ShapeDtypeStruct((n + 1, 2, 2 * order, 2 * order), jnp.bfloat16)
    full, one, last = pl.pallas_call(
        functools.partial(early_kernel, n, lats, slots),
        out_shape=(full, fields, fields),
        in_specs=[vmem] * 6,
        out_specs=(vmem,) * 3,
        scratch_shapes=[pltpu.VMEM((2, 2, 2 * tile, height), jnp.float32)],
        compiler_params=params,
        cost_estimate=pl.CostEstimate(flops=10**9, bytes_accessed=2 << 20, transcendentals=0),
    )(mine, near, mats, own_early, other_early, probe)
    keep, send = pl.pallas_call(
        functools.partial(main_kernel, n, lats, slots),
        out_shape=(jax.ShapeDtypeStruct(tiles, jnp.float32), jax.ShapeDtypeStruct(tiles, jnp.bfloat16)),
        in_specs=[vmem] * 10,
        out_specs=(vmem, vmem),
        scratch_shapes=[
            pltpu.VMEM((n, half, 2, order, order), jnp.float32),
            pltpu.VMEM((n, half, 2, order, order), jnp.float32),
            pltpu.VMEM((n - 2, 2, 2 * tile, height), jnp.float32),
        ],
        compiler_params=params,
        cost_estimate=pl.CostEstimate(flops=4 * 10**9, bytes_accessed=8 << 20, transcendentals=0),
    )(mine, near, full, own_late, other_late, probe, one, last, measured, near_measured)

    from_partner = lax.ppermute(send, AXES, partner)
    totals = [(keep[i] + from_partner[i].astype(jnp.float32)).astype(jnp.bfloat16) for i in range(n)]
    returned = [lax.ppermute(totals[i], AXES, [(d, s) for s, d in back_routes[a]]) for i, a in enumerate(back_turn)]
    returned = jnp.concatenate([r[None] for r in returned], axis=0)
    spot_first, spot_second = jnp.int32(0), jnp.int32(0)
    for i, a in enumerate(back_turn):
        spot_first = jnp.where(group == a, i, spot_first)
        spot_second = jnp.where(group == n - 1 - a, i, spot_second)
    from_first = lax.dynamic_index_in_dim(returned, spot_first, 0, False)
    from_first = jnp.where(group == first, totals[back_turn.index(first)], from_first)
    from_second = lax.dynamic_index_in_dim(returned, spot_second, 0, False).astype(jnp.float32)
    from_second = jnp.where(lat == 0, 0.0, from_second)
    return (from_first.astype(jnp.float32) + from_second)[:, None]


def solution(mesh):
    in_specs = (
        P(None, "beam", "lat", None),
        P(),
        P("lat"),
        P("lat"),
        P("lat"),
        P("lat", None, None),
    )
    out_specs = P(None, "beam", "lat", None)
    return jax.shard_map(
        on_device, mesh=mesh, in_specs=in_specs, out_specs=out_specs, check_vma=False
    )
```

```python
import functools
import math

import jax
import jax.numpy as jnp
import ml_dtypes
import numpy as np
from jax import lax
from jax.experimental import pallas as pl
from jax.experimental.pallas import tpu as pltpu
from jax.sharding import PartitionSpec as P

AXES = ("beam", "lat")


W_SCALE = 1.1775
LANES = 128


def matrices(order, steps):
    index = np.arange(order)
    dft = np.exp(-2j * np.pi * (index[:, None] * index[None, :] % order) / order) / math.sqrt(order)
    freq = (index + order // 2) % order - order // 2
    phase = np.exp(-1j * np.pi * (freq * freq % (4 * order)) / (2 * order))
    prop = (dft.conj() * phase) @ dft

    def pair(matrix):
        return np.stack([matrix.real, matrix.imag]).astype(ml_dtypes.bfloat16)

    def value(parts):
        parts = parts.astype(np.float64)
        return parts[0] + 1j * parts[1]

    out, ahead = [], np.zeros_like(prop)
    for step in range(steps):
        out.append(pair(prop - ahead))
        if step == steps - 1:
            out.append(pair(prop - ahead - value(out[-1])))
        else:
            ahead = ahead + value(out[-1]) - prop
    out.append(pair(W_SCALE * dft))
    return np.stack(out)


def place(n, lats, slice_index, short):
    first, second = n // 2 - 1, n // 2
    mirror = n - 1 - slice_index
    goals = {slice_index: first, mirror: second}
    outer = slice_index not in (first, second)
    if outer:
        goals[first] = min(slice_index, mirror)
        goals[second] = max(slice_index, mirror)
    to = {}
    for b in range(n):
        for l in range(lats):
            goal = goals.get(b, b)
            if goal == second:
                to[b, l] = (goal, (l - 1) % lats)
            else:
                to[b, l] = (goal, l ^ 1 if goal == b else l)
    if outer and short:
        via, middle = (first if goals[first] == mirror else second), lats // 4
        to[mirror, 0] = (mirror, middle)
        to[via, middle] = (second, lats - 1)
    return [(b * lats + l, c * lats + m) for (b, l), (c, m) in to.items()]


def swap(n, lats):
    return [(b * lats + l, b * lats + (l ^ 1)) for b in range(n) for l in range(lats)]


def turns(n, back):
    inner = list(range(1, n - 1))
    return [0] + inner[::-1] + [n - 1] if back else [n - 1, 0] + inner


def position(n, lats):
    group, lat = lax.axis_index("beam"), lax.axis_index("lat")
    side = lax.rem(lat, 2)
    at_first, at_second = group == n // 2 - 1, group == n // 2
    base = jnp.where(at_first, lat - side, lat + 1 - side)
    return lat, side, at_first, at_second, base


def corners(slots, local, side, mine_ref, near_ref):
    half = slots // 2
    values = jnp.where(local, mine_ref[...], near_ref[...])

    def scalar(i):
        return jnp.where(side == 0, values[0, i], values[0, i + half])

    return [scalar(s) for s in range(half)], [scalar(slots + s) for s in range(half)], values[0, 2 * slots]


def lay(ext_ref, k, own, other, row, beyond, tile):
    for value, r in ((own, row), (other, 1 - row)):
        value = value.astype(jnp.float32) * jnp.where(beyond & (r == 1), 0.0, 1.0)
        ext_ref[k, :, pl.ds(pl.multiple_of(r * tile, tile), tile), :] = value


def cut(ext_ref, k, c, xs, ys, order):
    sub = lax.broadcasted_iota(jnp.int32, (order // 8, 8, order), 1)
    lane = lax.broadcasted_iota(jnp.int32, (order + 8, order), 1)
    out = []
    for x, y in zip(xs, ys):
        turn = lax.rem(order - y, order)
        start = pl.ds(pl.multiple_of(x // 8 * 8, 8), order + 8)
        left = pltpu.roll(ext_ref[k, c, start, :order], turn, 1)
        right = pltpu.roll(ext_ref[k, c, start, order:], turn, 1)
        w = jnp.where(lane < order - y, left, right).reshape(order // 8 + 1, 8, order)
        r = lax.rem(x, 8)
        w = pltpu.roll(w, lax.rem(8 - r, 8), 1)
        out.append(jnp.where(sub < 8 - r, w[:-1], w[1:]).reshape(order, order))
    return out


def dot(a, b):
    return jnp.dot(a, b, preferred_element_type=jnp.float32)


def sandwich(full_ref, waves, ms, conj):
    order = waves[0][0].shape[0]
    right, left = (0, 1) if conj else (1, 0)
    rows = [jnp.concatenate(w, axis=1).astype(jnp.bfloat16) for w in waves]
    ys = [sum(dot(r, full_ref[m, right]) for m in ms).astype(jnp.bfloat16) for r in rows]
    cols = [jnp.concatenate([y[:, :order], y[:, order:]], axis=0) for y in ys]
    zs = [sum(dot(full_ref[m, left], c) for m in ms) for c in cols]
    return [(z[:order], z[order:]) for z in zs]


def step(n, i):
    return (n - 2, n - 1) if i == n - 2 else (i,)


def one_hot(order, tile, side, xs):
    tall = (2 * tile, order)
    index = lax.broadcasted_iota(jnp.int32, tall, 0)
    column = jnp.where(index >= tile, index - tile + (1 - side) * tile, index + side * tile)
    put_at = column - lax.broadcasted_iota(jnp.int32, tall, 1)
    return jnp.concatenate([jnp.where(put_at == x, 1.0, 0.0) for x in xs], axis=1).astype(jnp.bfloat16)


def placer(order, tile, puts_ref, ys):
    lane = lax.broadcasted_iota(jnp.int32, (order, order), 1)

    def put(values, keep_ref, send_ref, at):
        rows = []
        for y, value in zip(ys, values):
            value = pltpu.roll(value, lax.rem(y, order), 1)
            rows.append(
                jnp.concatenate(
                    [jnp.where(lane >= y, value, 0.0), jnp.where(lane < y, value, 0.0)], axis=1
                ).astype(jnp.bfloat16)
            )
        total = dot(puts_ref[...], jnp.concatenate(rows, axis=0))
        keep_ref[at] = total[:tile]
        send_ref[at] = total[tile:].astype(jnp.bfloat16)

    return put


def early_kernel(
    n, lats, slots, mine_ref, near_ref, mats_ref, own_ref, other_ref, probe_ref, full_ref, psi_ref, trn_ref, puts_ref,
    ext_ref,
):
    order, tile = probe_ref.shape[-1], own_ref.shape[2]
    lat, side, at_first, at_second, base = position(n, lats)
    xs, ys, count = corners(slots, base == lat, side, mine_ref, near_ref)
    puts_ref[...] = one_hot(order, tile, side, xs)
    for m in range(n + 1):
        re, im = mats_ref[m, 0], mats_ref[m, 1]
        for h, (upper, lower) in enumerate(((-im, im), (im, -im))):
            full_ref[m, h, :order, :order] = re
            full_ref[m, h, :order, order:] = upper
            full_ref[m, h, order:, :order] = lower
            full_ref[m, h, order:, order:] = re
    for k in range(2):
        i = jnp.where(at_second, k, 1 - k)
        lay(ext_ref, k, own_ref[i], other_ref[i], side, base + 1 >= lats, tile)
    first = [cut(ext_ref, 0, c, xs, ys, order) for c in range(2)]
    re, im = probe_ref[0], probe_ref[1]
    waves = []
    for c_re, c_im in zip(*first):
        t_re = 1.0 + c_re
        waves.append((t_re * re - c_im * im, t_re * im + c_im * re))
    waves = sandwich(full_ref, waves, step(n, 0), False)
    for s, wave in enumerate(waves):
        for c in range(2):
            psi_ref[s, c] = wave[c]
    for c in range(2):
        for s, value in enumerate(cut(ext_ref, 1, c, xs, ys, order)):
            trn_ref[s, c] = value


def main_kernel(
    n, lats, slots, mine_ref, near_ref, full_ref, own_ref, other_ref, probe_ref, one_ref, last_ref, puts_ref,
    meas_ref, near_meas_ref, keep_ref, send_ref, rows_ref, trn_ref, psi_ref, ext_ref,
):
    order, tile = probe_ref.shape[-1], own_ref.shape[2]
    half = slots // 2
    first = n // 2 - 1
    lat, side, at_first, at_second, base = position(n, lats)
    local = base == lat
    xs, ys, count = corners(slots, local, side, mine_ref, near_ref)
    put = placer(order, tile, puts_ref, ys)

    for k in range(1, n - 1):
        i = jnp.where(at_second, n - 2 - k, k - 1)
        row = jnp.where(at_first & (k == first), 1 - side, side)
        lay(ext_ref, k - 1, own_ref[i], other_ref[i], row, base + 1 >= lats, tile)

    waves = [(one_ref[s, 0], one_ref[s, 1]) for s in range(half)]
    for k in range(1, n):
        if k < n - 1:
            cuts = [cut(ext_ref, k - 1, c, xs, ys, order) for c in range(2)]
        else:
            cuts = [[last_ref[s, c] for s in range(half)] for c in range(2)]
        mult = []
        for s, (re, im) in enumerate(waves):
            psi_ref[k, s, 0] = re
            psi_ref[k, s, 1] = im
            t_re, t_im = 1.0 + cuts[0][s], cuts[1][s]
            trn_ref[k, s, 0] = t_re
            trn_ref[k, s, 1] = t_im
            mult.append((t_re * re - t_im * im, t_re * im + t_im * re))
        waves = sandwich(full_ref, mult, step(n, k) if k < n - 1 else (n,), False)

    mult = []
    for s, (re, im) in enumerate(waves):
        slot = side * half + s
        seen = jnp.where(local, meas_ref[slot], near_meas_ref[slot])
        misfit = jnp.where(slot < count, (re * re + im * im) * W_SCALE**-8 - seen * W_SCALE**-4, 0.0)
        mult.append((misfit * re, misfit * im))
    waves = sandwich(full_ref, mult, (n,), True)
    for k in reversed(range(1, n)):
        grad_re, grad_im, mult = [], [], []
        for s, (re, im) in enumerate(waves):
            p_re, p_im = psi_ref[k, s, 0], psi_ref[k, s, 1]
            grad_re.append(p_re * re + p_im * im)
            grad_im.append(p_re * im - p_im * re)
            t_re, t_im = trn_ref[k, s, 0], trn_ref[k, s, 1]
            mult.append((t_re * re + t_im * im, t_re * im - t_im * re))
        if k > 1:
            waves = sandwich(full_ref, mult, step(n, n - 1 - k), True)
        i = k - 1 if k == n - 1 else jnp.where(at_second, n - 2 - k, k - 1)
        put(grad_re, keep_ref, send_ref, (i, 0))
        put(grad_im, keep_ref, send_ref, (i, 1))
    for s, wave in enumerate(mult):
        for c in range(2):
            rows_ref[s, c] = wave[c].astype(jnp.bfloat16)


def first_slice_kernel(n, lats, slots, mine_ref, near_ref, full_ref, probe_ref, puts_ref, rows_ref, keep_ref, send_ref):
    order, tile = probe_ref.shape[-1], keep_ref.shape[1]
    lat, side, at_first, at_second, base = position(n, lats)
    xs, ys, count = corners(slots, base == lat, side, mine_ref, near_ref)
    put = placer(order, tile, puts_ref, ys)
    waves = [(rows_ref[s, 0], rows_ref[s, 1]) for s in range(slots // 2)]
    waves = sandwich(full_ref, waves, step(n, n - 2), True)
    p_re, p_im = probe_ref[0], probe_ref[1]
    put([p_re * re + p_im * im for re, im in waves], keep_ref, send_ref, 0)
    put([p_re * im - p_im * re for re, im in waves], keep_ref, send_ref, 1)


def on_device(contrast, probe, offset_x, offset_y, probe_count, measured):
    n, lats = lax.axis_size("beam"), lax.axis_size("lat")
    order, tile, height = probe.shape[1], contrast.shape[2], contrast.shape[3]
    slots = offset_x.shape[0]
    half = slots // 2
    first = n // 2 - 1
    lat, group = lax.axis_index("lat"), lax.axis_index("beam")
    routes = [place(n, lats, a, False) for a in range(n)]
    back_routes = [place(n, lats, a, True) for a in range(n)]
    turn, back_turn = turns(n, False), turns(n, True)
    partner = swap(n, lats)

    own_tile = contrast[:, 0].astype(jnp.bfloat16)[None]
    arrived = [lax.ppermute(own_tile, AXES, routes[a]) for a in turn]
    own_early = jnp.concatenate(arrived[:2], axis=0)
    own_late = jnp.concatenate(arrived[2:], axis=0)
    mine = jnp.concatenate([offset_x, offset_y, probe_count])
    mine = jnp.pad(mine, (0, LANES - mine.shape[0]))[None]
    near = lax.ppermute(mine, AXES, partner)
    near_measured = lax.ppermute(measured, AXES, partner)
    own_early, near = lax.optimization_barrier((own_early, near))
    other_early = lax.ppermute(own_early, AXES, partner)
    other_late = lax.ppermute(own_late, AXES, partner)

    vmem = pl.BlockSpec(memory_space=pltpu.VMEM)
    params = pltpu.CompilerParams(vmem_limit_bytes=(16 + 3 * n) << 20)
    mats = jnp.asarray(matrices(order, n - 1))
    tiles = (2, tile, height)
    fields = jax.ShapeDtypeStruct((half, 2, order, order), jnp.float32)
    full = jax.ShapeDtypeStruct((n + 1, 2, 2 * order, 2 * order), jnp.bfloat16)
    full, one, last, puts = pl.pallas_call(
        functools.partial(early_kernel, n, lats, slots),
        out_shape=(full, fields, fields, jax.ShapeDtypeStruct((2 * tile, half * order), jnp.bfloat16)),
        in_specs=[vmem] * 6,
        out_specs=(vmem,) * 4,
        scratch_shapes=[pltpu.VMEM((2, 2, 2 * tile, height), jnp.float32)],
        compiler_params=params,
        cost_estimate=pl.CostEstimate(flops=10**9, bytes_accessed=2 << 20, transcendentals=0),
    )(mine, near, mats, own_early, other_early, probe)
    keep, send, rows = pl.pallas_call(
        functools.partial(main_kernel, n, lats, slots),
        out_shape=(
            jax.ShapeDtypeStruct((n - 1,) + tiles, jnp.float32),
            jax.ShapeDtypeStruct((n - 1,) + tiles, jnp.bfloat16),
            jax.ShapeDtypeStruct((half, 2, order, order), jnp.bfloat16),
        ),
        in_specs=[vmem] * 11,
        out_specs=(vmem,) * 3,
        scratch_shapes=[
            pltpu.VMEM((n, half, 2, order, order), jnp.float32),
            pltpu.VMEM((n, half, 2, order, order), jnp.float32),
            pltpu.VMEM((n - 2, 2, 2 * tile, height), jnp.float32),
        ],
        compiler_params=params,
        cost_estimate=pl.CostEstimate(flops=4 * 10**9, bytes_accessed=8 << 20, transcendentals=0),
    )(mine, near, full, own_late, other_late, probe, one, last, puts, measured, near_measured)

    from_partner = lax.ppermute(send, AXES, partner)
    keep_first, send_first = pl.pallas_call(
        functools.partial(first_slice_kernel, n, lats, slots),
        out_shape=(jax.ShapeDtypeStruct(tiles, jnp.float32), jax.ShapeDtypeStruct(tiles, jnp.bfloat16)),
        in_specs=[vmem] * 6,
        out_specs=(vmem, vmem),
        compiler_params=params,
        cost_estimate=pl.CostEstimate(flops=10**9, bytes_accessed=2 << 20, transcendentals=0),
    )(mine, near, full, probe, puts, rows)
    from_partner_first = lax.ppermute(send_first, AXES, partner)
    totals = [(keep[i] + from_partner[i].astype(jnp.float32)).astype(jnp.bfloat16) for i in range(n - 1)]
    of_last = totals.pop()
    of_first = (keep_first + from_partner_first.astype(jnp.float32)).astype(jnp.bfloat16)
    at_second = group == n // 2
    totals = [jnp.where(at_second, of_last, of_first)] + totals + [jnp.where(at_second, of_first, of_last)]
    returned = [lax.ppermute(totals[a], AXES, [(d, s) for s, d in back_routes[a]]) for a in back_turn]
    returned = jnp.concatenate([r[None] for r in returned], axis=0)
    spot_first, spot_second = jnp.int32(0), jnp.int32(0)
    for i, a in enumerate(back_turn):
        spot_first = jnp.where(group == a, i, spot_first)
        spot_second = jnp.where(group == n - 1 - a, i, spot_second)
    from_first = lax.dynamic_index_in_dim(returned, spot_first, 0, False)
    from_first = jnp.where(group == first, totals[first], from_first)
    from_second = lax.dynamic_index_in_dim(returned, spot_second, 0, False).astype(jnp.float32)
    from_second = jnp.where(lat == 0, 0.0, from_second)
    return (from_first.astype(jnp.float32) + from_second)[:, None]


def solution(mesh):
    in_specs = (
        P(None, "beam", "lat", None),
        P(),
        P("lat"),
        P("lat"),
        P("lat"),
        P("lat", None, None),
    )
    out_specs = P(None, "beam", "lat", None)
    return jax.shard_map(
        on_device, mesh=mesh, in_specs=in_specs, out_specs=out_specs, check_vma=False
    )
```

```python
import functools
import math

import jax
import jax.numpy as jnp
import ml_dtypes
import numpy as np
from jax import lax
from jax.experimental import pallas as pl
from jax.experimental.pallas import tpu as pltpu
from jax.sharding import PartitionSpec as P

AXES = ("beam", "lat")


W_SCALE = 1.1775
LANES = 128


def matrices(order, steps):
    index = np.arange(order)
    dft = np.exp(-2j * np.pi * (index[:, None] * index[None, :] % order) / order) / math.sqrt(order)
    freq = (index + order // 2) % order - order // 2
    phase = np.exp(-1j * np.pi * (freq * freq % (4 * order)) / (2 * order))
    prop = (dft.conj() * phase) @ dft

    def pair(matrix):
        return np.stack([matrix.real, matrix.imag]).astype(ml_dtypes.bfloat16)

    def value(parts):
        parts = parts.astype(np.float64)
        return parts[0] + 1j * parts[1]

    out, ahead = [], np.zeros_like(prop)
    for step in range(steps):
        out.append(pair(prop - ahead))
        if step == steps - 1:
            out.append(pair(prop - ahead - value(out[-1])))
        else:
            ahead = ahead + value(out[-1]) - prop
    out.append(pair(W_SCALE * dft))
    return np.stack(out)


def place(n, lats, slice_index, short):
    first, second = n // 2 - 1, n // 2
    mirror = n - 1 - slice_index
    goals = {slice_index: first, mirror: second}
    outer = slice_index not in (first, second)
    if outer:
        goals[first] = min(slice_index, mirror)
        goals[second] = max(slice_index, mirror)
    to = {}
    for b in range(n):
        for l in range(lats):
            goal = goals.get(b, b)
            if goal == second:
                to[b, l] = (goal, (l - 1) % lats)
            else:
                to[b, l] = (goal, l ^ 1 if goal == b else l)
    if outer and short:
        via, middle = (first if goals[first] == mirror else second), lats // 4
        to[mirror, 0] = (mirror, middle)
        to[via, middle] = (second, lats - 1)
    return [(b * lats + l, c * lats + m) for (b, l), (c, m) in to.items()]


def swap(n, lats):
    return [(b * lats + l, b * lats + (l ^ 1)) for b in range(n) for l in range(lats)]


def turns(n, back):
    inner = list(range(1, n - 1))
    return [0] + inner[::-1] + [n - 1] if back else [n - 1, 0] + inner


def position(n, lats):
    group, lat = lax.axis_index("beam"), lax.axis_index("lat")
    side = lax.rem(lat, 2)
    at_first, at_second = group == n // 2 - 1, group == n // 2
    base = jnp.where(at_first, lat - side, lat + 1 - side)
    return lat, side, at_first, at_second, base


def corners(slots, local, side, mine_ref, near_ref):
    half = slots // 2
    values = jnp.where(local, mine_ref[...], near_ref[...])

    def scalar(i):
        return jnp.where(side == 0, values[0, i], values[0, i + half])

    return [scalar(s) for s in range(half)], [scalar(slots + s) for s in range(half)], values[0, 2 * slots]


def lay(ext_ref, k, own, other, row, beyond, tile):
    for value, r in ((own, row), (other, 1 - row)):
        value = value.astype(jnp.float32) * jnp.where(beyond & (r == 1), 0.0, 1.0)
        ext_ref[k, :, pl.ds(pl.multiple_of(r * tile, tile), tile), :] = value


def cut(ext_ref, k, c, xs, ys, order):
    sub = lax.broadcasted_iota(jnp.int32, (order // 8, 8, order), 1)
    lane = lax.broadcasted_iota(jnp.int32, (order + 8, order), 1)
    out = []
    for x, y in zip(xs, ys):
        turn = lax.rem(order - y, order)
        start = pl.ds(pl.multiple_of(x // 8 * 8, 8), order + 8)
        left = pltpu.roll(ext_ref[k, c, start, :order], turn, 1)
        right = pltpu.roll(ext_ref[k, c, start, order:], turn, 1)
        w = jnp.where(lane < order - y, left, right).reshape(order // 8 + 1, 8, order)
        r = lax.rem(x, 8)
        w = pltpu.roll(w, lax.rem(8 - r, 8), 1)
        out.append(jnp.where(sub < 8 - r, w[:-1], w[1:]).reshape(order, order))
    return out


def dot(a, b):
    return jnp.dot(a, b, preferred_element_type=jnp.float32)


def sandwich(full_ref, waves, ms, conj):
    order = waves[0][0].shape[0]
    right, left = (0, 1) if conj else (1, 0)
    rows = [jnp.concatenate(w, axis=1).astype(jnp.bfloat16) for w in waves]
    ys = [sum(dot(r, full_ref[m, right]) for m in ms).astype(jnp.bfloat16) for r in rows]
    cols = [jnp.concatenate([y[:, :order], y[:, order:]], axis=0) for y in ys]
    zs = [sum(dot(full_ref[m, left], c) for m in ms) for c in cols]
    return [(z[:order], z[order:]) for z in zs]


def step(n, i):
    return (n - 2, n - 1) if i == n - 2 else (i,)


def one_hot(order, tile, side, xs):
    tall = (2 * tile, order)
    index = lax.broadcasted_iota(jnp.int32, tall, 0)
    column = jnp.where(index >= tile, index - tile + (1 - side) * tile, index + side * tile)
    put_at = column - lax.broadcasted_iota(jnp.int32, tall, 1)
    return jnp.concatenate([jnp.where(put_at == x, 1.0, 0.0) for x in xs], axis=1).astype(jnp.bfloat16)


def placer(order, tile, puts_ref, ys):
    lane = lax.broadcasted_iota(jnp.int32, (order, order), 1)

    def put(values, keep_ref, send_ref, at):
        rows = []
        for y, value in zip(ys, values):
            value = pltpu.roll(value, lax.rem(y, order), 1)
            rows.append(
                jnp.concatenate(
                    [jnp.where(lane >= y, value, 0.0), jnp.where(lane < y, value, 0.0)], axis=1
                ).astype(jnp.bfloat16)
            )
        total = dot(puts_ref[...], jnp.concatenate(rows, axis=0))
        keep_ref[at] = total[:tile]
        send_ref[at] = total[tile:].astype(jnp.bfloat16)

    return put


def early_kernel(
    n, lats, slots, mine_ref, near_ref, mats_ref, own_ref, other_ref, probe_ref, full_ref, psi_ref, trn_ref, puts_ref,
    ext_ref,
):
    order, tile = probe_ref.shape[-1], own_ref.shape[2]
    lat, side, at_first, at_second, base = position(n, lats)
    xs, ys, count = corners(slots, base == lat, side, mine_ref, near_ref)
    def matrix(m):
        re, im = mats_ref[m, 0], mats_ref[m, 1]
        for h, (upper, lower) in enumerate(((-im, im), (im, -im))):
            full_ref[m, h, :order, :order] = re
            full_ref[m, h, :order, order:] = upper
            full_ref[m, h, order:, :order] = lower
            full_ref[m, h, order:, order:] = re

    def tiles(k):
        i = jnp.where(at_second, k, 1 - k)
        lay(ext_ref, k, own_ref[i], other_ref[i], side, base + 1 >= lats, tile)

    matrix(0)
    tiles(0)
    first = [cut(ext_ref, 0, c, xs, ys, order) for c in range(2)]
    re, im = probe_ref[0], probe_ref[1]
    waves = []
    for c_re, c_im in zip(*first):
        t_re = 1.0 + c_re
        waves.append((t_re * re - c_im * im, t_re * im + c_im * re))
    waves = sandwich(full_ref, waves, step(n, 0), False)
    tiles(1)
    for c in range(2):
        for s, value in enumerate(cut(ext_ref, 1, c, xs, ys, order)):
            trn_ref[s, c] = value
    for m in range(1, n + 1):
        matrix(m)
    puts_ref[...] = one_hot(order, tile, side, xs)
    for s, wave in enumerate(waves):
        for c in range(2):
            psi_ref[s, c] = wave[c]


def main_kernel(
    n, lats, slots, mine_ref, near_ref, full_ref, own_ref, other_ref, probe_ref, one_ref, last_ref, puts_ref,
    meas_ref, near_meas_ref, keep_ref, send_ref, rows_ref, trn_ref, psi_ref, ext_ref,
):
    order, tile = probe_ref.shape[-1], own_ref.shape[2]
    half = slots // 2
    first = n // 2 - 1
    lat, side, at_first, at_second, base = position(n, lats)
    local = base == lat
    xs, ys, count = corners(slots, local, side, mine_ref, near_ref)
    put = placer(order, tile, puts_ref, ys)

    for k in range(1, n - 1):
        i = jnp.where(at_second, n - 2 - k, k - 1)
        row = jnp.where(at_first & (k == first), 1 - side, side)
        lay(ext_ref, k - 1, own_ref[i], other_ref[i], row, base + 1 >= lats, tile)

    waves = [(one_ref[s, 0], one_ref[s, 1]) for s in range(half)]
    for k in range(1, n):
        if k < n - 1:
            cuts = [cut(ext_ref, k - 1, c, xs, ys, order) for c in range(2)]
        else:
            cuts = [[last_ref[s, c] for s in range(half)] for c in range(2)]
        mult = []
        for s, (re, im) in enumerate(waves):
            psi_ref[k, s, 0] = re
            psi_ref[k, s, 1] = im
            t_re, t_im = 1.0 + cuts[0][s], cuts[1][s]
            trn_ref[k, s, 0] = t_re
            trn_ref[k, s, 1] = t_im
            mult.append((t_re * re - t_im * im, t_re * im + t_im * re))
        waves = sandwich(full_ref, mult, step(n, k) if k < n - 1 else (n,), False)

    mult = []
    for s, (re, im) in enumerate(waves):
        slot = side * half + s
        seen = jnp.where(local, meas_ref[slot], near_meas_ref[slot])
        misfit = jnp.where(slot < count, (re * re + im * im) * W_SCALE**-8 - seen * W_SCALE**-4, 0.0)
        mult.append((misfit * re, misfit * im))
    waves = sandwich(full_ref, mult, (n,), True)
    for k in reversed(range(1, n)):
        grad_re, grad_im, mult = [], [], []
        for s, (re, im) in enumerate(waves):
            p_re, p_im = psi_ref[k, s, 0], psi_ref[k, s, 1]
            grad_re.append(p_re * re + p_im * im)
            grad_im.append(p_re * im - p_im * re)
            t_re, t_im = trn_ref[k, s, 0], trn_ref[k, s, 1]
            mult.append((t_re * re + t_im * im, t_re * im - t_im * re))
        if k > 1:
            waves = sandwich(full_ref, mult, step(n, n - 1 - k), True)
        i = k - 1 if k == n - 1 else jnp.where(at_second, n - 2 - k, k - 1)
        put(grad_re, keep_ref, send_ref, (i, 0))
        put(grad_im, keep_ref, send_ref, (i, 1))
    for s, wave in enumerate(mult):
        for c in range(2):
            rows_ref[s, c] = wave[c].astype(jnp.bfloat16)


def first_slice_kernel(n, lats, slots, mine_ref, near_ref, full_ref, probe_ref, puts_ref, rows_ref, keep_ref, send_ref):
    order, tile = probe_ref.shape[-1], keep_ref.shape[1]
    lat, side, at_first, at_second, base = position(n, lats)
    xs, ys, count = corners(slots, base == lat, side, mine_ref, near_ref)
    put = placer(order, tile, puts_ref, ys)
    waves = [(rows_ref[s, 0], rows_ref[s, 1]) for s in range(slots // 2)]
    waves = sandwich(full_ref, waves, step(n, n - 2), True)
    p_re, p_im = probe_ref[0], probe_ref[1]
    put([p_re * re + p_im * im for re, im in waves], keep_ref, send_ref, 0)
    put([p_re * im - p_im * re for re, im in waves], keep_ref, send_ref, 1)


def on_device(contrast, probe, offset_x, offset_y, probe_count, measured):
    n, lats = lax.axis_size("beam"), lax.axis_size("lat")
    order, tile, height = probe.shape[1], contrast.shape[2], contrast.shape[3]
    slots = offset_x.shape[0]
    half = slots // 2
    first = n // 2 - 1
    lat, group = lax.axis_index("lat"), lax.axis_index("beam")
    routes = [place(n, lats, a, False) for a in range(n)]
    back_routes = [place(n, lats, a, True) for a in range(n)]
    turn, back_turn = turns(n, False), turns(n, True)
    partner = swap(n, lats)

    own_tile = contrast[:, 0].astype(jnp.bfloat16)[None]
    arrived = [lax.ppermute(own_tile, AXES, routes[a]) for a in turn]
    own_early = jnp.concatenate(arrived[:2], axis=0)
    own_late = jnp.concatenate(arrived[2:], axis=0)
    mine = jnp.concatenate([offset_x, offset_y, probe_count])
    mine = jnp.pad(mine, (0, LANES - mine.shape[0]))[None]
    near = lax.ppermute(mine, AXES, partner)
    near_measured = lax.ppermute(measured, AXES, partner)
    own_early, near = lax.optimization_barrier((own_early, near))
    other_early = lax.ppermute(own_early, AXES, partner)
    other_late = lax.ppermute(own_late, AXES, partner)

    vmem = pl.BlockSpec(memory_space=pltpu.VMEM)
    params = pltpu.CompilerParams(vmem_limit_bytes=(16 + 3 * n) << 20)
    mats = jnp.asarray(matrices(order, n - 1))
    tiles = (2, tile, height)
    fields = jax.ShapeDtypeStruct((half, 2, order, order), jnp.float32)
    full = jax.ShapeDtypeStruct((n + 1, 2, 2 * order, 2 * order), jnp.bfloat16)
    full, one, last, puts = pl.pallas_call(
        functools.partial(early_kernel, n, lats, slots),
        out_shape=(full, fields, fields, jax.ShapeDtypeStruct((2 * tile, half * order), jnp.bfloat16)),
        in_specs=[vmem] * 6,
        out_specs=(vmem,) * 4,
        scratch_shapes=[pltpu.VMEM((2, 2, 2 * tile, height), jnp.float32)],
        compiler_params=params,
        cost_estimate=pl.CostEstimate(flops=10**9, bytes_accessed=2 << 20, transcendentals=0),
    )(mine, near, mats, own_early, other_early, probe)
    keep, send, rows = pl.pallas_call(
        functools.partial(main_kernel, n, lats, slots),
        out_shape=(
            jax.ShapeDtypeStruct((n - 1,) + tiles, jnp.float32),
            jax.ShapeDtypeStruct((n - 1,) + tiles, jnp.bfloat16),
            jax.ShapeDtypeStruct((half, 2, order, order), jnp.bfloat16),
        ),
        in_specs=[vmem] * 11,
        out_specs=(vmem,) * 3,
        scratch_shapes=[
            pltpu.VMEM((n, half, 2, order, order), jnp.float32),
            pltpu.VMEM((n, half, 2, order, order), jnp.float32),
            pltpu.VMEM((n - 2, 2, 2 * tile, height), jnp.float32),
        ],
        compiler_params=params,
        cost_estimate=pl.CostEstimate(flops=4 * 10**9, bytes_accessed=8 << 20, transcendentals=0),
    )(mine, near, full, own_late, other_late, probe, one, last, puts, measured, near_measured)

    from_partner = lax.ppermute(send, AXES, partner)
    keep_first, send_first = pl.pallas_call(
        functools.partial(first_slice_kernel, n, lats, slots),
        out_shape=(jax.ShapeDtypeStruct(tiles, jnp.float32), jax.ShapeDtypeStruct(tiles, jnp.bfloat16)),
        in_specs=[vmem] * 6,
        out_specs=(vmem, vmem),
        compiler_params=params,
        cost_estimate=pl.CostEstimate(flops=10**9, bytes_accessed=2 << 20, transcendentals=0),
    )(mine, near, full, probe, puts, rows)
    from_partner_first = lax.ppermute(send_first, AXES, partner)
    totals = [(keep[i] + from_partner[i].astype(jnp.float32)).astype(jnp.bfloat16) for i in range(n - 1)]
    of_last = totals.pop()
    of_first = (keep_first + from_partner_first.astype(jnp.float32)).astype(jnp.bfloat16)
    at_second = group == n // 2
    totals = [jnp.where(at_second, of_last, of_first)] + totals + [jnp.where(at_second, of_first, of_last)]
    returned = [lax.ppermute(totals[a], AXES, [(d, s) for s, d in back_routes[a]]) for a in back_turn]
    returned = jnp.concatenate([r[None] for r in returned], axis=0)
    spot_first, spot_second = jnp.int32(0), jnp.int32(0)
    for i, a in enumerate(back_turn):
        spot_first = jnp.where(group == a, i, spot_first)
        spot_second = jnp.where(group == n - 1 - a, i, spot_second)
    from_first = lax.dynamic_index_in_dim(returned, spot_first, 0, False)
    from_first = jnp.where(group == first, totals[first], from_first)
    from_second = lax.dynamic_index_in_dim(returned, spot_second, 0, False).astype(jnp.float32)
    from_second = jnp.where(lat == 0, 0.0, from_second)
    return (from_first.astype(jnp.float32) + from_second)[:, None]


def solution(mesh):
    in_specs = (
        P(None, "beam", "lat", None),
        P(),
        P("lat"),
        P("lat"),
        P("lat"),
        P("lat", None, None),
    )
    out_specs = P(None, "beam", "lat", None)
    return jax.shard_map(
        on_device, mesh=mesh, in_specs=in_specs, out_specs=out_specs, check_vma=False
    )
```

```python
import functools
import math

import jax
import jax.numpy as jnp
import ml_dtypes
import numpy as np
from jax import lax
from jax.experimental import pallas as pl
from jax.experimental.pallas import tpu as pltpu
from jax.sharding import PartitionSpec as P

AXES = ("beam", "lat")


W_SCALE = 1.1775
LANES = 128


def matrices(order, steps):
    index = np.arange(order)
    dft = np.exp(-2j * np.pi * (index[:, None] * index[None, :] % order) / order) / math.sqrt(order)
    freq = (index + order // 2) % order - order // 2
    phase = np.exp(-1j * np.pi * (freq * freq % (4 * order)) / (2 * order))
    prop = (dft.conj() * phase) @ dft

    def pair(matrix):
        return np.stack([matrix.real, matrix.imag]).astype(ml_dtypes.bfloat16)

    def value(parts):
        parts = parts.astype(np.float64)
        return parts[0] + 1j * parts[1]

    out, ahead = [], np.zeros_like(prop)
    for step in range(steps):
        out.append(pair(prop - ahead))
        if step == steps - 1:
            out.append(pair(prop - ahead - value(out[-1])))
        else:
            ahead = ahead + value(out[-1]) - prop
    out.append(pair(W_SCALE * dft))
    return np.stack(out)


def place(n, lats, slice_index, short):
    first, second = n // 2 - 1, n // 2
    mirror = n - 1 - slice_index
    goals = {slice_index: first, mirror: second}
    outer = slice_index not in (first, second)
    if outer:
        goals[first] = min(slice_index, mirror)
        goals[second] = max(slice_index, mirror)
    to = {}
    for b in range(n):
        for l in range(lats):
            goal = goals.get(b, b)
            if goal == second:
                to[b, l] = (goal, (l - 1) % lats)
            else:
                to[b, l] = (goal, l ^ 1 if goal == b else l)
    if outer and short:
        via, middle = (first if goals[first] == mirror else second), lats // 4
        to[mirror, 0] = (mirror, middle)
        to[via, middle] = (second, lats - 1)
    return [(b * lats + l, c * lats + m) for (b, l), (c, m) in to.items()]


def swap(n, lats):
    return [(b * lats + l, b * lats + (l ^ 1)) for b in range(n) for l in range(lats)]


def turns(n, back):
    inner = list(range(1, n - 1))
    return [0] + inner[::-1] + [n - 1] if back else [n - 1, 0] + inner


def position(n, lats):
    group, lat = lax.axis_index("beam"), lax.axis_index("lat")
    side = lax.rem(lat, 2)
    at_first, at_second = group == n // 2 - 1, group == n // 2
    base = jnp.where(at_first, lat - side, lat + 1 - side)
    return lat, side, at_first, at_second, base


def corners(slots, local, side, mine_ref, near_ref):
    half = slots // 2
    values = jnp.where(local, mine_ref[...], near_ref[...])

    def scalar(i):
        return jnp.where(side == 0, values[0, i], values[0, i + half])

    return [scalar(s) for s in range(half)], [scalar(slots + s) for s in range(half)], values[0, 2 * slots]


def lay(ext_ref, k, own, other, row, beyond, tile):
    for value, r in ((own, row), (other, 1 - row)):
        value = value.astype(jnp.float32) * jnp.where(beyond & (r == 1), 0.0, 1.0)
        ext_ref[k, :, pl.ds(pl.multiple_of(r * tile, tile), tile), :] = value


def cut(ext_ref, k, c, xs, ys, order):
    sub = lax.broadcasted_iota(jnp.int32, (order // 8, 8, order), 1)
    lane = lax.broadcasted_iota(jnp.int32, (order + 8, order), 1)
    out = []
    for x, y in zip(xs, ys):
        turn = lax.rem(order - y, order)
        start = pl.ds(pl.multiple_of(x // 8 * 8, 8), order + 8)
        left = pltpu.roll(ext_ref[k, c, start, :order], turn, 1)
        right = pltpu.roll(ext_ref[k, c, start, order:], turn, 1)
        w = jnp.where(lane < order - y, left, right).reshape(order // 8 + 1, 8, order)
        r = lax.rem(x, 8)
        w = pltpu.roll(w, lax.rem(8 - r, 8), 1)
        out.append(jnp.where(sub < 8 - r, w[:-1], w[1:]).reshape(order, order))
    return out


def dot(a, b):
    return jnp.dot(a, b, preferred_element_type=jnp.float32)


def sandwich(full_ref, waves, ms, conj):
    order = waves[0][0].shape[0]
    right, left = (0, 1) if conj else (1, 0)
    rows = [jnp.concatenate(w, axis=1).astype(jnp.bfloat16) for w in waves]
    ys = [sum(dot(r, full_ref[m, right]) for m in ms).astype(jnp.bfloat16) for r in rows]
    cols = [jnp.concatenate([y[:, :order], y[:, order:]], axis=0) for y in ys]
    zs = [sum(dot(full_ref[m, left], c) for m in ms) for c in cols]
    return [(z[:order], z[order:]) for z in zs]


def step(n, i):
    return (n - 2, n - 1) if i == n - 2 else (i,)


def one_hot(order, tile, side, xs):
    tall = (2 * tile, order)
    index = lax.broadcasted_iota(jnp.int32, tall, 0)
    column = jnp.where(index >= tile, index - tile + (1 - side) * tile, index + side * tile)
    put_at = column - lax.broadcasted_iota(jnp.int32, tall, 1)
    return jnp.concatenate([jnp.where(put_at == x, 1.0, 0.0) for x in xs], axis=1).astype(jnp.bfloat16)


def placer(order, tile, puts_ref, ys):
    lane = lax.broadcasted_iota(jnp.int32, (order, order), 1)

    def put(values, keep_ref, send_ref, at):
        rows = []
        for y, value in zip(ys, values):
            value = pltpu.roll(value, lax.rem(y, order), 1)
            rows.append(
                jnp.concatenate(
                    [jnp.where(lane >= y, value, 0.0), jnp.where(lane < y, value, 0.0)], axis=1
                ).astype(jnp.bfloat16)
            )
        total = dot(puts_ref[...], jnp.concatenate(rows, axis=0))
        keep_ref[at] = total[:tile]
        send_ref[at] = total[tile:].astype(jnp.bfloat16)

    return put


def early_kernel(
    n, lats, slots, mine_ref, near_ref, mats_ref, own_ref, other_ref, probe_ref, full_ref, psi_ref, trn_ref, puts_ref,
    ext_ref,
):
    order, tile = probe_ref.shape[-1], own_ref.shape[2]
    lat, side, at_first, at_second, base = position(n, lats)
    xs, ys, count = corners(slots, base == lat, side, mine_ref, near_ref)
    def matrix(m):
        re, im = mats_ref[m, 0], mats_ref[m, 1]
        for h, (upper, lower) in enumerate(((-im, im), (im, -im))):
            full_ref[m, h, :order, :order] = re
            full_ref[m, h, :order, order:] = upper
            full_ref[m, h, order:, :order] = lower
            full_ref[m, h, order:, order:] = re

    def tiles(k):
        i = jnp.where(at_second, k, 1 - k)
        lay(ext_ref, k, own_ref[i], other_ref[i], side, base + 1 >= lats, tile)

    matrix(0)
    tiles(0)
    first = [cut(ext_ref, 0, c, xs, ys, order) for c in range(2)]
    re, im = probe_ref[0], probe_ref[1]
    waves = []
    for c_re, c_im in zip(*first):
        t_re = 1.0 + c_re
        waves.append((t_re * re - c_im * im, t_re * im + c_im * re))
    waves = sandwich(full_ref, waves, step(n, 0), False)
    tiles(1)
    for c in range(2):
        for s, value in enumerate(cut(ext_ref, 1, c, xs, ys, order)):
            trn_ref[s, c] = value
    for m in range(1, n + 1):
        matrix(m)
    puts_ref[...] = one_hot(order, tile, side, xs)
    for s, wave in enumerate(waves):
        for c in range(2):
            psi_ref[s, c] = wave[c]


def main_kernel(
    n, lats, slots, mine_ref, near_ref, full_ref, own_ref, other_ref, probe_ref, one_ref, last_ref, puts_ref,
    meas_ref, near_meas_ref, keep_ref, send_ref, rows_ref, trn_ref, psi_ref, ext_ref,
):
    order, tile = probe_ref.shape[-1], own_ref.shape[2]
    half = slots // 2
    first = n // 2 - 1
    lat, side, at_first, at_second, base = position(n, lats)
    local = base == lat
    xs, ys, count = corners(slots, local, side, mine_ref, near_ref)
    put = placer(order, tile, puts_ref, ys)

    for k in range(1, n - 1):
        i = jnp.where(at_second, n - 2 - k, k - 1)
        row = jnp.where(at_first & (k == first), 1 - side, side)
        lay(ext_ref, k - 1, own_ref[i], other_ref[i], row, base + 1 >= lats, tile)

    waves = [(one_ref[s, 0], one_ref[s, 1]) for s in range(half)]
    for k in range(1, n):
        if k < n - 1:
            cuts = [cut(ext_ref, k - 1, c, xs, ys, order) for c in range(2)]
        else:
            cuts = [[last_ref[s, c] for s in range(half)] for c in range(2)]
        mult = []
        for s, (re, im) in enumerate(waves):
            t_re, t_im = 1.0 + cuts[0][s], cuts[1][s]
            if k > 1:
                psi_ref[k, s, 0] = re
                psi_ref[k, s, 1] = im
            if k < n - 1:
                trn_ref[k, s, 0] = t_re
                trn_ref[k, s, 1] = t_im
            mult.append((t_re * re - t_im * im, t_re * im + t_im * re))
        waves = sandwich(full_ref, mult, step(n, k) if k < n - 1 else (n,), False)

    mult = []
    for s, (re, im) in enumerate(waves):
        slot = side * half + s
        seen = jnp.where(local, meas_ref[slot], near_meas_ref[slot])
        misfit = jnp.where(slot < count, (re * re + im * im) * W_SCALE**-8 - seen * W_SCALE**-4, 0.0)
        mult.append((misfit * re, misfit * im))
    waves = sandwich(full_ref, mult, (n,), True)
    for k in reversed(range(1, n)):
        grad_re, grad_im, mult = [], [], []
        for s, (re, im) in enumerate(waves):
            p_re, p_im = (psi_ref[k, s, 0], psi_ref[k, s, 1]) if k > 1 else (one_ref[s, 0], one_ref[s, 1])
            grad_re.append(p_re * re + p_im * im)
            grad_im.append(p_re * im - p_im * re)
            if k < n - 1:
                t_re, t_im = trn_ref[k, s, 0], trn_ref[k, s, 1]
            else:
                t_re, t_im = 1.0 + last_ref[s, 0], last_ref[s, 1]
            mult.append((t_re * re + t_im * im, t_re * im - t_im * re))
        if k > 1:
            waves = sandwich(full_ref, mult, step(n, n - 1 - k), True)
        i = k - 1 if k == n - 1 else jnp.where(at_second, n - 2 - k, k - 1)
        put(grad_re, keep_ref, send_ref, (i, 0))
        put(grad_im, keep_ref, send_ref, (i, 1))
    for s, wave in enumerate(mult):
        for c in range(2):
            rows_ref[s, c] = wave[c].astype(jnp.bfloat16)


def first_slice_kernel(n, lats, slots, mine_ref, near_ref, full_ref, probe_ref, puts_ref, rows_ref, keep_ref, send_ref):
    order, tile = probe_ref.shape[-1], keep_ref.shape[1]
    lat, side, at_first, at_second, base = position(n, lats)
    xs, ys, count = corners(slots, base == lat, side, mine_ref, near_ref)
    put = placer(order, tile, puts_ref, ys)
    waves = [(rows_ref[s, 0], rows_ref[s, 1]) for s in range(slots // 2)]
    waves = sandwich(full_ref, waves, step(n, n - 2), True)
    p_re, p_im = probe_ref[0], probe_ref[1]
    put([p_re * re + p_im * im for re, im in waves], keep_ref, send_ref, 0)
    put([p_re * im - p_im * re for re, im in waves], keep_ref, send_ref, 1)


def on_device(contrast, probe, offset_x, offset_y, probe_count, measured):
    n, lats = lax.axis_size("beam"), lax.axis_size("lat")
    order, tile, height = probe.shape[1], contrast.shape[2], contrast.shape[3]
    slots = offset_x.shape[0]
    half = slots // 2
    first = n // 2 - 1
    lat, group = lax.axis_index("lat"), lax.axis_index("beam")
    routes = [place(n, lats, a, False) for a in range(n)]
    back_routes = [place(n, lats, a, True) for a in range(n)]
    turn, back_turn = turns(n, False), turns(n, True)
    partner = swap(n, lats)

    own_tile = contrast[:, 0].astype(jnp.bfloat16)[None]
    arrived = [lax.ppermute(own_tile, AXES, routes[a]) for a in turn]
    own_early = jnp.concatenate(arrived[:2], axis=0)
    own_late = jnp.concatenate(arrived[2:], axis=0)
    mine = jnp.concatenate([offset_x, offset_y, probe_count])
    mine = jnp.pad(mine, (0, LANES - mine.shape[0]))[None]
    near = lax.ppermute(mine, AXES, partner)
    near_measured = lax.ppermute(measured, AXES, partner)
    own_early, near = lax.optimization_barrier((own_early, near))
    other_early = lax.ppermute(own_early, AXES, partner)
    other_late = lax.ppermute(own_late, AXES, partner)

    vmem = pl.BlockSpec(memory_space=pltpu.VMEM)
    params = pltpu.CompilerParams(vmem_limit_bytes=(16 + 3 * n) << 20)
    mats = jnp.asarray(matrices(order, n - 1))
    tiles = (2, tile, height)
    fields = jax.ShapeDtypeStruct((half, 2, order, order), jnp.float32)
    full = jax.ShapeDtypeStruct((n + 1, 2, 2 * order, 2 * order), jnp.bfloat16)
    full, one, last, puts = pl.pallas_call(
        functools.partial(early_kernel, n, lats, slots),
        out_shape=(full, fields, fields, jax.ShapeDtypeStruct((2 * tile, half * order), jnp.bfloat16)),
        in_specs=[vmem] * 6,
        out_specs=(vmem,) * 4,
        scratch_shapes=[pltpu.VMEM((2, 2, 2 * tile, height), jnp.float32)],
        compiler_params=params,
        cost_estimate=pl.CostEstimate(flops=10**9, bytes_accessed=2 << 20, transcendentals=0),
    )(mine, near, mats, own_early, other_early, probe)
    keep, send, rows = pl.pallas_call(
        functools.partial(main_kernel, n, lats, slots),
        out_shape=(
            jax.ShapeDtypeStruct((n - 1,) + tiles, jnp.float32),
            jax.ShapeDtypeStruct((n - 1,) + tiles, jnp.bfloat16),
            jax.ShapeDtypeStruct((half, 2, order, order), jnp.bfloat16),
        ),
        in_specs=[vmem] * 11,
        out_specs=(vmem,) * 3,
        scratch_shapes=[
            pltpu.VMEM((n, half, 2, order, order), jnp.float32),
            pltpu.VMEM((n, half, 2, order, order), jnp.float32),
            pltpu.VMEM((n - 2, 2, 2 * tile, height), jnp.float32),
        ],
        compiler_params=params,
        cost_estimate=pl.CostEstimate(flops=4 * 10**9, bytes_accessed=8 << 20, transcendentals=0),
    )(mine, near, full, own_late, other_late, probe, one, last, puts, measured, near_measured)

    from_partner = lax.ppermute(send, AXES, partner)
    keep_first, send_first = pl.pallas_call(
        functools.partial(first_slice_kernel, n, lats, slots),
        out_shape=(jax.ShapeDtypeStruct(tiles, jnp.float32), jax.ShapeDtypeStruct(tiles, jnp.bfloat16)),
        in_specs=[vmem] * 6,
        out_specs=(vmem, vmem),
        compiler_params=params,
        cost_estimate=pl.CostEstimate(flops=10**9, bytes_accessed=2 << 20, transcendentals=0),
    )(mine, near, full, probe, puts, rows)
    from_partner_first = lax.ppermute(send_first, AXES, partner)
    totals = [(keep[i] + from_partner[i].astype(jnp.float32)).astype(jnp.bfloat16) for i in range(n - 1)]
    of_last = totals.pop()
    of_first = (keep_first + from_partner_first.astype(jnp.float32)).astype(jnp.bfloat16)
    at_second = group == n // 2
    totals = [jnp.where(at_second, of_last, of_first)] + totals + [jnp.where(at_second, of_first, of_last)]
    returned = [lax.ppermute(totals[a], AXES, [(d, s) for s, d in back_routes[a]]) for a in back_turn]
    returned = jnp.concatenate([r[None] for r in returned], axis=0)
    spot_first, spot_second = jnp.int32(0), jnp.int32(0)
    for i, a in enumerate(back_turn):
        spot_first = jnp.where(group == a, i, spot_first)
        spot_second = jnp.where(group == n - 1 - a, i, spot_second)
    from_first = lax.dynamic_index_in_dim(returned, spot_first, 0, False)
    from_first = jnp.where(group == first, totals[first], from_first)
    from_second = lax.dynamic_index_in_dim(returned, spot_second, 0, False).astype(jnp.float32)
    from_second = jnp.where(lat == 0, 0.0, from_second)
    return (from_first.astype(jnp.float32) + from_second)[:, None]


def solution(mesh):
    in_specs = (
        P(None, "beam", "lat", None),
        P(),
        P("lat"),
        P("lat"),
        P("lat"),
        P("lat", None, None),
    )
    out_specs = P(None, "beam", "lat", None)
    return jax.shard_map(
        on_device, mesh=mesh, in_specs=in_specs, out_specs=out_specs, check_vma=False
    )
```

```python
import functools
import math

import jax
import jax.numpy as jnp
import ml_dtypes
import numpy as np
from jax import lax
from jax.experimental import pallas as pl
from jax.experimental.pallas import tpu as pltpu
from jax.sharding import PartitionSpec as P

AXES = ("beam", "lat")


W_SCALE = 1.1775
LANES = 128


def matrices(order, steps):
    index = np.arange(order)
    dft = np.exp(-2j * np.pi * (index[:, None] * index[None, :] % order) / order) / math.sqrt(order)
    freq = (index + order // 2) % order - order // 2
    phase = np.exp(-1j * np.pi * (freq * freq % (4 * order)) / (2 * order))
    prop = (dft.conj() * phase) @ dft

    def pair(matrix):
        return np.stack([matrix.real, matrix.imag]).astype(ml_dtypes.bfloat16)

    def value(parts):
        parts = parts.astype(np.float64)
        return parts[0] + 1j * parts[1]

    out, ahead = [], np.zeros_like(prop)
    for step in range(steps):
        out.append(pair(prop - ahead))
        if step == steps - 1:
            out.append(pair(prop - ahead - value(out[-1])))
        else:
            ahead = ahead + value(out[-1]) - prop
    out.append(pair(W_SCALE * dft))
    return np.stack(out)


def place(n, lats, slice_index, short):
    first, second = n // 2 - 1, n // 2
    mirror = n - 1 - slice_index
    goals = {slice_index: first, mirror: second}
    outer = slice_index not in (first, second)
    if outer:
        goals[first] = min(slice_index, mirror)
        goals[second] = max(slice_index, mirror)
    to = {}
    for b in range(n):
        for l in range(lats):
            goal = goals.get(b, b)
            if goal == second:
                to[b, l] = (goal, (l - 1) % lats)
            else:
                to[b, l] = (goal, l ^ 1 if goal == b else l)
    if outer and short:
        via, middle = (first if goals[first] == mirror else second), lats // 4
        to[mirror, 0] = (mirror, middle)
        to[via, middle] = (second, lats - 1)
    return [(b * lats + l, c * lats + m) for (b, l), (c, m) in to.items()]


def swap(n, lats):
    return [(b * lats + l, b * lats + (l ^ 1)) for b in range(n) for l in range(lats)]


def turns(n, back):
    inner = list(range(1, n - 1))
    return [0] + inner[::-1] + [n - 1] if back else [n - 1, 0] + inner


def position(n, lats):
    group, lat = lax.axis_index("beam"), lax.axis_index("lat")
    side = lax.rem(lat, 2)
    at_first, at_second = group == n // 2 - 1, group == n // 2
    base = jnp.where(at_first, lat - side, lat + 1 - side)
    return lat, side, at_first, at_second, base


def corners(slots, local, side, mine_ref, near_ref):
    half = slots // 2
    values = jnp.where(local, mine_ref[...], near_ref[...])

    def scalar(i):
        return jnp.where(side == 0, values[0, i], values[0, i + half])

    return [scalar(s) for s in range(half)], [scalar(slots + s) for s in range(half)], values[0, 2 * slots]


def lay(ext_ref, k, own, other, row, beyond, tile):
    for value, r in ((own, row), (other, 1 - row)):
        value = value.astype(jnp.float32) * jnp.where(beyond & (r == 1), 0.0, 1.0)
        ext_ref[k, :, pl.ds(pl.multiple_of(r * tile, tile), tile), :] = value


def cut(ext_ref, k, c, xs, ys, order):
    sub = lax.broadcasted_iota(jnp.int32, (order // 8, 8, order), 1)
    lane = lax.broadcasted_iota(jnp.int32, (order + 8, order), 1)
    out = []
    for x, y in zip(xs, ys):
        turn = lax.rem(order - y, order)
        start = pl.ds(pl.multiple_of(x // 8 * 8, 8), order + 8)
        left = pltpu.roll(ext_ref[k, c, start, :order], turn, 1)
        right = pltpu.roll(ext_ref[k, c, start, order:], turn, 1)
        w = jnp.where(lane < order - y, left, right).reshape(order // 8 + 1, 8, order)
        r = lax.rem(x, 8)
        w = pltpu.roll(w, lax.rem(8 - r, 8), 1)
        out.append(jnp.where(sub < 8 - r, w[:-1], w[1:]).reshape(order, order))
    return out


def dot(a, b):
    return jnp.dot(a, b, preferred_element_type=jnp.float32)


def sandwich(full_ref, waves, ms, conj):
    order = waves[0][0].shape[0]
    right, left = (0, 1) if conj else (1, 0)
    rows = [jnp.concatenate(w, axis=1).astype(jnp.bfloat16) for w in waves]
    ys = [sum(dot(r, full_ref[m, right]) for m in ms).astype(jnp.bfloat16) for r in rows]
    cols = [jnp.concatenate([y[:, :order], y[:, order:]], axis=0) for y in ys]
    zs = [sum(dot(full_ref[m, left], c) for m in ms) for c in cols]
    return [(z[:order], z[order:]) for z in zs]


def step(n, i):
    return (n - 2, n - 1) if i == n - 2 else (i,)


def one_hot(order, tile, side, xs):
    tall = (2 * tile, order)
    index = lax.broadcasted_iota(jnp.int32, tall, 0)
    column = jnp.where(index >= tile, index - tile + (1 - side) * tile, index + side * tile)
    put_at = column - lax.broadcasted_iota(jnp.int32, tall, 1)
    return jnp.concatenate([jnp.where(put_at == x, 1.0, 0.0) for x in xs], axis=1).astype(jnp.bfloat16)


def placer(order, tile, puts_ref, ys):
    lane = lax.broadcasted_iota(jnp.int32, (order, order), 1)

    def put(values, keep_ref, send_ref, at):
        rows = []
        for y, value in zip(ys, values):
            value = pltpu.roll(value, lax.rem(y, order), 1)
            rows.append(
                jnp.concatenate(
                    [jnp.where(lane >= y, value, 0.0), jnp.where(lane < y, value, 0.0)], axis=1
                ).astype(jnp.bfloat16)
            )
        total = dot(puts_ref[...], jnp.concatenate(rows, axis=0))
        keep_ref[at] = total[:tile].astype(jnp.bfloat16)
        send_ref[at] = total[tile:].astype(jnp.bfloat16)

    return put


def early_kernel(
    n, lats, slots, mine_ref, near_ref, mats_ref, own_ref, other_ref, probe_ref, full_ref, psi_ref, trn_ref, puts_ref,
    ext_ref,
):
    order, tile = probe_ref.shape[-1], own_ref.shape[2]
    lat, side, at_first, at_second, base = position(n, lats)
    xs, ys, count = corners(slots, base == lat, side, mine_ref, near_ref)
    def matrix(m):
        re, im = mats_ref[m, 0], mats_ref[m, 1]
        for h, (upper, lower) in enumerate(((-im, im), (im, -im))):
            full_ref[m, h, :order, :order] = re
            full_ref[m, h, :order, order:] = upper
            full_ref[m, h, order:, :order] = lower
            full_ref[m, h, order:, order:] = re

    def tiles(k):
        i = jnp.where(at_second, k, 1 - k)
        lay(ext_ref, k, own_ref[i], other_ref[i], side, base + 1 >= lats, tile)

    matrix(0)
    tiles(0)
    first = [cut(ext_ref, 0, c, xs, ys, order) for c in range(2)]
    re, im = probe_ref[0], probe_ref[1]
    waves = []
    for c_re, c_im in zip(*first):
        t_re = 1.0 + c_re
        waves.append((t_re * re - c_im * im, t_re * im + c_im * re))
    waves = sandwich(full_ref, waves, step(n, 0), False)
    tiles(1)
    for c in range(2):
        for s, value in enumerate(cut(ext_ref, 1, c, xs, ys, order)):
            trn_ref[s, c] = value
    for m in range(1, n + 1):
        matrix(m)
    puts_ref[...] = one_hot(order, tile, side, xs)
    for s, wave in enumerate(waves):
        for c in range(2):
            psi_ref[s, c] = wave[c]


def main_kernel(
    n, lats, slots, mine_ref, near_ref, full_ref, own_ref, other_ref, probe_ref, one_ref, last_ref, puts_ref,
    meas_ref, near_meas_ref, keep_ref, send_ref, rows_ref, trn_ref, psi_ref, ext_ref,
):
    order, tile = probe_ref.shape[-1], own_ref.shape[2]
    half = slots // 2
    first = n // 2 - 1
    lat, side, at_first, at_second, base = position(n, lats)
    local = base == lat
    xs, ys, count = corners(slots, local, side, mine_ref, near_ref)
    put = placer(order, tile, puts_ref, ys)

    for k in range(1, n - 1):
        i = jnp.where(at_second, n - 2 - k, k - 1)
        row = jnp.where(at_first & (k == first), 1 - side, side)
        lay(ext_ref, k - 1, own_ref[i], other_ref[i], row, base + 1 >= lats, tile)

    waves = [(one_ref[s, 0], one_ref[s, 1]) for s in range(half)]
    for k in range(1, n):
        if k < n - 1:
            cuts = [cut(ext_ref, k - 1, c, xs, ys, order) for c in range(2)]
        else:
            cuts = [[last_ref[s, c] for s in range(half)] for c in range(2)]
        mult = []
        for s, (re, im) in enumerate(waves):
            psi_ref[k, s, 0] = re
            psi_ref[k, s, 1] = im
            t_re, t_im = 1.0 + cuts[0][s], cuts[1][s]
            trn_ref[k, s, 0] = t_re
            trn_ref[k, s, 1] = t_im
            mult.append((t_re * re - t_im * im, t_re * im + t_im * re))
        waves = sandwich(full_ref, mult, step(n, k) if k < n - 1 else (n,), False)

    mult = []
    for s, (re, im) in enumerate(waves):
        slot = side * half + s
        seen = jnp.where(local, meas_ref[slot], near_meas_ref[slot])
        misfit = jnp.where(slot < count, (re * re + im * im) * W_SCALE**-8 - seen * W_SCALE**-4, 0.0)
        mult.append((misfit * re, misfit * im))
    waves = sandwich(full_ref, mult, (n,), True)
    for k in reversed(range(1, n)):
        grad_re, grad_im, mult = [], [], []
        for s, (re, im) in enumerate(waves):
            p_re, p_im = psi_ref[k, s, 0], psi_ref[k, s, 1]
            grad_re.append(p_re * re + p_im * im)
            grad_im.append(p_re * im - p_im * re)
            t_re, t_im = trn_ref[k, s, 0], trn_ref[k, s, 1]
            mult.append((t_re * re + t_im * im, t_re * im - t_im * re))
        if k > 1:
            waves = sandwich(full_ref, mult, step(n, n - 1 - k), True)
        i = k - 1 if k == n - 1 else jnp.where(at_second, n - 2 - k, k - 1)
        put(grad_re, keep_ref, send_ref, (i, 0))
        put(grad_im, keep_ref, send_ref, (i, 1))
    for s, wave in enumerate(mult):
        for c in range(2):
            rows_ref[s, c] = wave[c].astype(jnp.bfloat16)


def first_slice_kernel(n, lats, slots, mine_ref, near_ref, full_ref, probe_ref, puts_ref, rows_ref, keep_ref, send_ref):
    order, tile = probe_ref.shape[-1], keep_ref.shape[1]
    lat, side, at_first, at_second, base = position(n, lats)
    xs, ys, count = corners(slots, base == lat, side, mine_ref, near_ref)
    put = placer(order, tile, puts_ref, ys)
    waves = [(rows_ref[s, 0], rows_ref[s, 1]) for s in range(slots // 2)]
    waves = sandwich(full_ref, waves, step(n, n - 2), True)
    p_re, p_im = probe_ref[0], probe_ref[1]
    put([p_re * re + p_im * im for re, im in waves], keep_ref, send_ref, 0)
    put([p_re * im - p_im * re for re, im in waves], keep_ref, send_ref, 1)


def on_device(contrast, probe, offset_x, offset_y, probe_count, measured):
    n, lats = lax.axis_size("beam"), lax.axis_size("lat")
    order, tile, height = probe.shape[1], contrast.shape[2], contrast.shape[3]
    slots = offset_x.shape[0]
    half = slots // 2
    first = n // 2 - 1
    lat, group = lax.axis_index("lat"), lax.axis_index("beam")
    routes = [place(n, lats, a, False) for a in range(n)]
    back_routes = [place(n, lats, a, True) for a in range(n)]
    turn, back_turn = turns(n, False), turns(n, True)
    partner = swap(n, lats)

    own_tile = contrast[:, 0].astype(jnp.bfloat16)[None]
    arrived = [lax.ppermute(own_tile, AXES, routes[a]) for a in turn]
    own_early = jnp.concatenate(arrived[:2], axis=0)
    own_late = jnp.concatenate(arrived[2:], axis=0)
    mine = jnp.concatenate([offset_x, offset_y, probe_count])
    mine = jnp.pad(mine, (0, LANES - mine.shape[0]))[None]
    near = lax.ppermute(mine, AXES, partner)
    near_measured = lax.ppermute(measured, AXES, partner)
    own_early, near = lax.optimization_barrier((own_early, near))
    other_early = lax.ppermute(own_early, AXES, partner)
    other_late = lax.ppermute(own_late, AXES, partner)

    vmem = pl.BlockSpec(memory_space=pltpu.VMEM)
    params = pltpu.CompilerParams(vmem_limit_bytes=(16 + 3 * n) << 20)
    mats = jnp.asarray(matrices(order, n - 1))
    tiles = (2, tile, height)
    fields = jax.ShapeDtypeStruct((half, 2, order, order), jnp.float32)
    full = jax.ShapeDtypeStruct((n + 1, 2, 2 * order, 2 * order), jnp.bfloat16)
    full, one, last, puts = pl.pallas_call(
        functools.partial(early_kernel, n, lats, slots),
        out_shape=(full, fields, fields, jax.ShapeDtypeStruct((2 * tile, half * order), jnp.bfloat16)),
        in_specs=[vmem] * 6,
        out_specs=(vmem,) * 4,
        scratch_shapes=[pltpu.VMEM((2, 2, 2 * tile, height), jnp.float32)],
        compiler_params=params,
        cost_estimate=pl.CostEstimate(flops=10**9, bytes_accessed=2 << 20, transcendentals=0),
    )(mine, near, mats, own_early, other_early, probe)
    keep, send, rows = pl.pallas_call(
        functools.partial(main_kernel, n, lats, slots),
        out_shape=(
            jax.ShapeDtypeStruct((n - 1,) + tiles, jnp.bfloat16),
            jax.ShapeDtypeStruct((n - 1,) + tiles, jnp.bfloat16),
            jax.ShapeDtypeStruct((half, 2, order, order), jnp.bfloat16),
        ),
        in_specs=[vmem] * 11,
        out_specs=(vmem,) * 3,
        scratch_shapes=[
            pltpu.VMEM((n, half, 2, order, order), jnp.float32),
            pltpu.VMEM((n, half, 2, order, order), jnp.float32),
            pltpu.VMEM((n - 2, 2, 2 * tile, height), jnp.float32),
        ],
        compiler_params=params,
        cost_estimate=pl.CostEstimate(flops=4 * 10**9, bytes_accessed=8 << 20, transcendentals=0),
    )(mine, near, full, own_late, other_late, probe, one, last, puts, measured, near_measured)

    from_partner = lax.ppermute(send, AXES, partner)
    keep_first, send_first = pl.pallas_call(
        functools.partial(first_slice_kernel, n, lats, slots),
        out_shape=(jax.ShapeDtypeStruct(tiles, jnp.bfloat16), jax.ShapeDtypeStruct(tiles, jnp.bfloat16)),
        in_specs=[vmem] * 6,
        out_specs=(vmem, vmem),
        compiler_params=params,
        cost_estimate=pl.CostEstimate(flops=10**9, bytes_accessed=2 << 20, transcendentals=0),
    )(mine, near, full, probe, puts, rows)
    from_partner_first = lax.ppermute(send_first, AXES, partner)
    totals = [(keep[i].astype(jnp.float32) + from_partner[i].astype(jnp.float32)).astype(jnp.bfloat16) for i in range(n - 1)]
    of_last = totals.pop()
    of_first = (keep_first.astype(jnp.float32) + from_partner_first.astype(jnp.float32)).astype(jnp.bfloat16)
    at_second = group == n // 2
    totals = [jnp.where(at_second, of_last, of_first)] + totals + [jnp.where(at_second, of_first, of_last)]
    returned = [lax.ppermute(totals[a], AXES, [(d, s) for s, d in back_routes[a]]) for a in back_turn]
    returned = jnp.concatenate([r[None] for r in returned], axis=0)
    spot_first, spot_second = jnp.int32(0), jnp.int32(0)
    for i, a in enumerate(back_turn):
        spot_first = jnp.where(group == a, i, spot_first)
        spot_second = jnp.where(group == n - 1 - a, i, spot_second)
    from_first = lax.dynamic_index_in_dim(returned, spot_first, 0, False)
    from_first = jnp.where(group == first, totals[first], from_first)
    from_second = lax.dynamic_index_in_dim(returned, spot_second, 0, False).astype(jnp.float32)
    from_second = jnp.where(lat == 0, 0.0, from_second)
    return (from_first.astype(jnp.float32) + from_second)[:, None]


def solution(mesh):
    in_specs = (
        P(None, "beam", "lat", None),
        P(),
        P("lat"),
        P("lat"),
        P("lat"),
        P("lat", None, None),
    )
    out_specs = P(None, "beam", "lat", None)
    return jax.shard_map(
        on_device, mesh=mesh, in_specs=in_specs, out_specs=out_specs, check_vma=False
    )
```
